256 devices in a mesh: tile: 16 (over y, x), cand: 1, group: 16 (over z, core).
Axes of the slice: x: 4, y: 4, z: 8, core: 2. Of those that a mesh axis runs over, the one named last changes fastest.
Arguments:
- latent: bfloat16 [64, 48, 48, 384], P(('cand', 'group'), 'tile'), may hold values from -6 to 6
- gain_first: float32 [384], replicated, may hold values from 0.25 to 1.75
- weight_first: bfloat16 [3, 3, 1152, 384], P(None, None, 'group'), may hold values from -0.0625 to 0.0625
- bias_first: float32 [384], replicated, may hold values from -0.6 to 0.6
- gain_second: float32 [384], replicated, may hold values from 0.25 to 1.75
- weight_second: bfloat16 [3, 3, 1152, 384], P(None, None, 'group'), may hold values from -0.0625 to 0.0625
- bias_second: float32 [384], replicated, may hold values from -0.6 to 0.6
Outputs:
- decoded: bfloat16 [64, 48, 48, 384], P(('cand', 'group'), 'tile')
The draws below stay inside these ranges and needn't reach their ends.
All inputs are finite; a program needn't handle non-finite values.
Results may differ from the reference program's by a relative error of at most 0.0042.
Values may be sent and summed in bfloat16 or wider, within the bound.
No kernel may reach another device: no remote copies, remote signals or barrier semaphores. Data moves between devices by JAX's collectives and lax.ppermute only.
A program may use at most 128 MiB of HBM per device.

```python
import jax
import jax.numpy as jnp
from jax import lax

C = 384
WID = 48
FRAMES = 64
ROWS = 48


def level_of(own_key, dims, shards, low, top_value):
    loudness, own = 1.0, jax.random.fold_in(own_key, 6)
    for axis_at, parts in shards:
        heights = jnp.exp(jax.random.uniform(jax.random.fold_in(own, axis_at), (parts,), jnp.float32, low / len(shards), top_value / len(shards)))
        loudness = loudness * jnp.repeat(heights, dims[axis_at] // parts).reshape([-1 if axis == axis_at else 1 for axis in range(len(dims))])
    return loudness


def scatter_about(key, extent, scale, most, split=(), dtype=jnp.bfloat16):
    level = level_of(key, extent, split, -0.22, 0.18) if split else 1.0
    array = jax.random.normal(key, extent, jnp.float32) * scale * level
    return jnp.minimum(jnp.maximum(array, -most), most).astype(dtype)


def setup_inputs(seed: int = 0, part: int = 0) -> dict:
    streams_of = jax.random.split(jax.random.key(seed), 8)
    part_keys = jax.random.split(jax.random.fold_in(streams_of[7], part), 8)
    return {
        "latent": scatter_about(part_keys[0], (FRAMES, ROWS, WID, C), 1.0, 6.0, ((0, 16), (1, 16))),
        "gain_first": jnp.clip(1.0 + 0.15 * jax.random.normal(streams_of[1], (C,), jnp.float32), 0.25, 1.75),
        "weight_first": scatter_about(streams_of[2], (3, 3, 3 * C, C), (27 * C) ** -0.5, 0.0625, ((2, 16),)),
        "bias_first": jnp.clip(jax.random.uniform(streams_of[3], (C,), jnp.float32, -0.6, 0.6), -0.6, 0.6),
        "gain_second": jnp.clip(1.0 + 0.15 * jax.random.normal(streams_of[4], (C,), jnp.float32), 0.25, 1.75),
        "weight_second": scatter_about(streams_of[5], (3, 3, 3 * C, C), (27 * C) ** -0.5, 0.0625, ((2, 16),)),
        "bias_second": jnp.clip(jax.random.uniform(streams_of[6], (C,), jnp.float32, -0.6, 0.6), -0.6, 0.6),
    }


def activate(values, gain):
    wide = values.astype(jnp.float32)
    scaled = wide * jax.lax.rsqrt(lax.optimization_barrier(jnp.mean(wide * wide, axis=-1, keepdims=True)) + 1e-06) * gain
    return jax.nn.silu(scaled)

def taps(padded, weight):
    count = padded.shape[0] - 2
    tall = padded.shape[1] - 2
    across = padded.shape[2] - 2
    chans = padded.shape[3]
    total = jnp.zeros((count * tall * across, weight.shape[3]), jnp.float32)
    for step_t in range(3):
        for step_r in range(3):
            window = padded[step_t:step_t + count, step_r:step_r + tall]
            joined = jnp.concatenate([window[:, :, k:k + across] for k in range(3)], axis=-1)
            joined = joined.reshape(-1, 3 * chans).astype(jnp.float32)
            total = total + jnp.dot(joined, weight[step_t, step_r].astype(jnp.float32), preferred_element_type=jnp.float32)
    return total.reshape(count, tall, across, weight.shape[3])

def reference(latent, gain_first, weight_first, bias_first, gain_second, weight_second, bias_second):
    first = activate(latent, gain_first).astype(jnp.bfloat16)
    padded = jnp.pad(first, ((2, 0), (1, 1), (1, 1), (0, 0)))
    hidden = taps(padded, weight_first) + bias_first
    second = activate(hidden, gain_second).astype(jnp.bfloat16)
    padded = jnp.pad(second, ((2, 0), (1, 1), (1, 1), (0, 0)))
    result = latent.astype(jnp.float32) + taps(padded, weight_second) + bias_second
    return result.astype(jnp.bfloat16)
```

```python
import functools

import jax
import jax.numpy as jnp
from jax import lax
from jax.experimental import pallas as pl
from jax.experimental.pallas import tpu as pltpu
from jax.sharding import Mesh
from jax.sharding import PartitionSpec as P

BF = jnp.bfloat16
F32 = jnp.float32
C = 384
NY, NX, NZ = 4, 4, 8
AXES = ("y", "x", "z", "c")
SLAB = 144
PIECE = 16
UNIT = SLAB + PIECE


def index(y, x, z, c):
    return ((y % NY * NX + x % NX) * NZ + z % NZ) * 2 + c


def perm(to):
    return [
        (index(y, x, z, c), index(*to(y, x, z, c)))
        for y in range(NY)
        for x in range(NX)
        for z in range(NZ)
        for c in range(2)
    ]


def along_z(steps):
    return perm(lambda y, x, z, c: (y, x, z + steps if c == 0 else z - steps, c))


Z1, Z2 = along_z(1), along_z(2)
SWAP = perm(lambda y, x, z, c: (y, x, z, 1 - c))
RING_UP = perm(lambda y, x, z, c: (y, x + 1, z, c) if c == 0 else (y + 1, x, z, c))
RING_DOWN = perm(lambda y, x, z, c: (y, x - 1, z, c) if c == 0 else (y - 1, x, z, c))


def neighbours(tile_step, group_step):
    tiles, groups = NY * NX, NZ * 2
    return [
        (t * groups + g, (t + tile_step) * groups + g + group_step)
        for t in range(tiles)
        for g in range(groups)
        if 0 <= t + tile_step < tiles and 0 <= g + group_step < groups
    ]


def send(value, pairs):
    return lax.ppermute(value, AXES, pairs)


def activate(values, gain):
    wide = values.astype(F32)
    scaled = wide * lax.rsqrt(jnp.mean(wide * wide, axis=-1, keepdims=True) + 1e-06) * gain
    return jax.nn.silu(scaled)


def grow(own):
    tail = own[2:]
    above = send(own[:, 2:], neighbours(1, 0))
    below = send(own[:, :1], neighbours(-1, 0))
    earlier = send(tail, neighbours(0, 1))
    corner_above = send(tail[:, 2:], neighbours(1, 1))
    corner_below = send(tail[:, :1], neighbours(-1, 1))
    return jnp.concatenate(
        [
            jnp.concatenate([corner_above, earlier, corner_below], axis=1),
            jnp.concatenate([above, own, below], axis=1),
        ],
        axis=0,
    )


def gather(weight, core, tap_x, tap_y):
    first_core = core == 0
    other = send(weight, SWAP)
    slab = jnp.concatenate(
        [jnp.where(first_core, weight, other), jnp.where(first_core, other, weight)], axis=1
    )

    def unit(tap):
        whole = lax.dynamic_slice_in_dim(slab, tap, 1, axis=0)[0]
        piece = lax.dynamic_slice_in_dim(slab[0], (tap - 1) * PIECE, PIECE, axis=0)
        return jnp.concatenate([whole, piece], axis=0)

    both = jnp.concatenate([unit(tap_x), unit(tap_y), slab[0, 8 * PIECE :]], axis=0)
    one = send(both, Z1)
    two = send(both, Z2)
    three = send(two, Z1)
    half = jnp.where(first_core, two[:UNIT], two[UNIT : 2 * UNIT])
    four = send(jnp.concatenate([half, two[2 * UNIT :]], axis=0), Z2)
    other_one, other_two, other_three = (send(v, SWAP) for v in (one, two, three))
    other_four = send(four, SWAP)

    def mine(value):
        return jnp.where(first_core, value[:UNIT], value[UNIT : 2 * UNIT])

    def ring(chunk):
        cut = (chunk.shape[0] + 1) // 2
        up, down = send(chunk, RING_UP), send(chunk, RING_DOWN)
        far_up, far_down = send(up[:cut], RING_UP), send(down[cut:], RING_DOWN)
        others = [send(v, SWAP) for v in (up, down, far_up, far_down)]
        return [up, down, far_up, far_down], others

    near = ring(jnp.stack([mine(one), mine(other_one), mine(two), mine(other_two)]))
    far = ring(jnp.stack([mine(three), mine(other_three), four[:UNIT]]))
    direct = [one, other_one, two, other_two, three, other_three]
    return [slab, *direct, four, other_four, *near[0], *near[1], *far[0], *far[1]]


def conv_kernel(second, where, grown, *refs):
    arrays, rest = refs[:25], refs[25:]
    (extra, gain, bias, out, whole, joined, total, sems) = rest
    slab, direct, four, other_four = arrays[0], arrays[1:7], arrays[7], arrays[8]
    near, other_near, far, other_far = arrays[9:13], arrays[13:17], arrays[17:21], arrays[21:25]
    z, sign = where[8], where[9]

    def at(offset):
        return lax.rem(z + offset + 2 * NZ, NZ)

    copies = []

    def fetch(src, dst):
        copy = pltpu.make_async_copy(src, dst, sems.at[len(copies)])
        copy.start()
        copies.append(copy)
        return copy

    def fetch_unit(src, start, tap, spot):
        piece = pl.ds(pl.multiple_of((tap - 1) * PIECE, PIECE), PIECE)
        return [
            fetch(src.at[pl.ds(start, SLAB)], whole.at[tap, spot]),
            fetch(src.at[pl.ds(start + SLAB, PIECE)], whole.at[0, spot, piece]),
        ]

    def last_piece(src, start, spot):
        return fetch(src.at[pl.ds(start, PIECE)], whole.at[0, spot, pl.ds(8 * PIECE, PIECE)])

    own = fetch(slab, whole.at[:, z])
    needs = [[] for _ in range(9)]
    order = [where[k] for k in range(8)]
    for step, (src, other) in enumerate(zip(direct[::2], direct[1::2]), start=1):
        for ref, spot in ((src, at(sign * step)), (other, at(-sign * step))):
            for k in range(2):
                needs[k] += fetch_unit(ref, k * UNIT, where[10 + k], spot)
            needs[8].append(last_piece(ref, 2 * UNIT, spot))
    spot = at(4)
    needs[1] += fetch_unit(four, 0, order[0], spot)
    needs[1] += fetch_unit(other_four, 0, order[1], spot)
    needs[8].append(last_piece(four, UNIT, spot))

    def fetch_ring(near, far, turn, base):
        nears = [turn, -turn, 2 * turn, -2 * turn]
        fars = [3 * turn, -3 * turn, 4]
        for group, offsets in ((near, nears), (far, fars)):
            cut = (len(offsets) + 1) // 2
            up, down, far_up, far_down = group
            for k, offset in enumerate(offsets):
                needs[base] += fetch_unit(up.at[k], 0, order[base], at(offset))
                needs[base + 1] += fetch_unit(down.at[k], 0, order[base + 1], at(offset))
                src = far_up.at[k] if k < cut else far_down.at[k - cut]
                needs[base + 2] += fetch_unit(src, 0, order[base + 2], at(offset))

    fetch_ring(near, far, sign, 2)
    fetch_ring(other_near, other_far, -sign, 5)

    for f in range(6):
        for r in range(5):
            line = grown[f, r].astype(F32)
            column = lax.broadcasted_iota(jnp.int32, line.shape, 0)
            before = jnp.where(column == 0, 0.0, pltpu.roll(line, 1, 0))
            after = jnp.where(column == 47, 0.0, pltpu.roll(line, 47, 0))
            joined[f, r, :, :C] = before.astype(BF)
            joined[f, r, :, C : 2 * C] = grown[f, r]
            joined[f, r, :, 2 * C :] = after.astype(BF)

    total[...] = jnp.zeros_like(total)

    def add(tap):
        window = joined[pl.ds(lax.div(tap, 3), 4), pl.ds(lax.rem(tap, 3), 3)]
        total[...] += jnp.dot(
            window.reshape(576, 3 * C),
            whole[tap].reshape(NZ * SLAB, C),
            preferred_element_type=F32,
        )

    own.wait()
    for copy in needs[0] + needs[1]:
        copy.wait()
    add(where[10])
    add(where[11])
    for k in range(2, 8):
        for copy in needs[k]:
            copy.wait()
        add(order[k])
    for copy in needs[8]:
        copy.wait()
    add(0)

    hidden = total[...] + bias[...]
    if second:
        result = hidden + extra[...].astype(F32)
    else:
        result = activate(hidden, gain[...])
    out[...] = result.astype(BF)


def conv(grown, pieces, extra, gain, bias, where, second):
    any_spec = pl.BlockSpec(memory_space=pl.ANY)
    vmem = pl.BlockSpec(memory_space=pltpu.VMEM)
    out = pl.pallas_call(
        functools.partial(conv_kernel, second),
        out_shape=jax.ShapeDtypeStruct((576, C), BF),
        in_specs=[pl.BlockSpec(memory_space=pltpu.SMEM), vmem, *[any_spec] * 25, vmem, vmem, vmem],
        out_specs=vmem,
        scratch_shapes=[
            pltpu.VMEM((9, NZ, SLAB, C), BF),
            pltpu.VMEM((6, 5, 48, 3 * C), BF),
            pltpu.VMEM((576, C), F32),
            pltpu.SemaphoreType.DMA((160,)),
        ],
        compiler_params=pltpu.CompilerParams(vmem_limit_bytes=32 * 2**20),
        cost_estimate=pl.CostEstimate(
            flops=2 * 576 * 9 * 3 * C * C, bytes_accessed=9 * 3 * C * C * 2, transcendentals=0
        ),
        name="conv_second" if second else "conv_first",
    )(where, grown, *pieces, extra, gain, bias)
    return out.reshape(4, 3, 48, C)


def local(latent, gain_first, weight_first, bias_first, gain_second, weight_second, bias_second):
    y, x, z, core = (lax.axis_index(name) for name in AXES)
    tap_x, tap_y = 1 + x, 5 + y

    def taps(step):
        across, down = 1 + lax.rem(x + step + NX, NX), 5 + lax.rem(y + step + NY, NY)
        return jnp.where(core == 0, across, down), jnp.where(core == 0, down, across)

    mine, other = zip(*(taps(step) for step in (0, -1, 1, 2)))
    where = jnp.stack(
        [mine[0], other[0], *mine[1:], *other[1:], z, jnp.where(core == 0, -1, 1), tap_x, tap_y]
    ).astype(jnp.int32)

    first = activate(latent, gain_first).astype(BF)
    weights_first = gather(weight_first.reshape(9, 72, C), core, tap_x, tap_y)
    weights_second = gather(weight_second.reshape(9, 72, C), core, tap_x, tap_y)
    flat = latent.reshape(576, C)
    row = lambda v: v.reshape(1, C)
    second = conv(grow(first), weights_first, flat, row(gain_second), row(bias_first), where, False)
    return conv(grow(second), weights_second, flat, row(gain_second), row(bias_second), where, True)


def solution(mesh):
    fine = Mesh(mesh.devices.reshape(NY, NX, NZ, 2), AXES)
    frames = P(("z", "c"), ("y", "x"), None, None)
    slices = P(None, None, ("z", "c"), None)
    return jax.shard_map(
        local,
        mesh=fine,
        in_specs=(frames, P(), slices, P(), P(), slices, P()),
        out_specs=frames,
        check_vma=False,
    )
```

```python
import functools

import jax
import jax.numpy as jnp
from jax import lax
from jax.experimental import pallas as pl
from jax.experimental.pallas import tpu as pltpu
from jax.sharding import Mesh
from jax.sharding import PartitionSpec as P

BF = jnp.bfloat16
F32 = jnp.float32
C = 384
NY, NX, NZ = 4, 4, 8
AXES = ("y", "x", "z", "c")
SLAB = 144
PIECE = 16
UNIT = SLAB + PIECE


def index(y, x, z, c):
    return ((y % NY * NX + x % NX) * NZ + z % NZ) * 2 + c


def perm(to):
    return [
        (index(y, x, z, c), index(*to(y, x, z, c)))
        for y in range(NY)
        for x in range(NX)
        for z in range(NZ)
        for c in range(2)
    ]


def along_z(steps):
    return perm(lambda y, x, z, c: (y, x, z + steps if c == 0 else z - steps, c))


Z1, Z2 = along_z(1), along_z(2)
SWAP = perm(lambda y, x, z, c: (y, x, z, 1 - c))
RING_UP = perm(lambda y, x, z, c: (y, x + 1, z, c) if c == 0 else (y + 1, x, z, c))
RING_DOWN = perm(lambda y, x, z, c: (y, x - 1, z, c) if c == 0 else (y - 1, x, z, c))


def neighbours(tile_step, group_step):
    tiles, groups = NY * NX, NZ * 2
    return [
        (t * groups + g, (t + tile_step) * groups + g + group_step)
        for t in range(tiles)
        for g in range(groups)
        if 0 <= t + tile_step < tiles and 0 <= g + group_step < groups
    ]


def send(value, pairs):
    return lax.ppermute(value, AXES, pairs)


def activate(values, gain):
    wide = values.astype(F32)
    scaled = wide * lax.rsqrt(jnp.mean(wide * wide, axis=-1, keepdims=True) + 1e-06) * gain
    return jax.nn.silu(scaled)


def grow(own):
    tail = own[2:]
    above = send(own[:, 2:], neighbours(1, 0))
    below = send(own[:, :1], neighbours(-1, 0))
    earlier = send(tail, neighbours(0, 1))
    corner_above = send(tail[:, 2:], neighbours(1, 1))
    corner_below = send(tail[:, :1], neighbours(-1, 1))
    return jnp.concatenate(
        [
            jnp.concatenate([corner_above, earlier, corner_below], axis=1),
            jnp.concatenate([above, own, below], axis=1),
        ],
        axis=0,
    )


def after(value, *others):
    return lax.optimization_barrier((value, others))[0]


class Gather:
    def __init__(self, weight, core, tap_x, tap_y):
        self.first_core = core == 0
        other = send(weight, SWAP)
        self.low = jnp.where(self.first_core, weight, other)
        self.high = jnp.where(self.first_core, other, weight)
        self.slab = jnp.concatenate([self.low, self.high], axis=1)
        self.taps = tap_x, tap_y

    def unit(self, tap):
        whole = lax.dynamic_slice_in_dim(self.slab, tap, 1, axis=0)[0]
        piece = lax.dynamic_slice_in_dim(self.slab[0], (tap - 1) * PIECE, PIECE, axis=0)
        return jnp.concatenate([whole, piece], axis=0)

    def start(self):
        return jnp.concatenate([*map(self.unit, self.taps), self.slab[0, 8 * PIECE :]], axis=0)

    def mine(self, value):
        return jnp.where(self.first_core, value[:UNIT], value[UNIT : 2 * UNIT])

    def hop(self, both):
        self.one, self.two = send(both, Z1), send(both, Z2)
        self.other_one, self.other_two = send(self.one, SWAP), send(self.two, SWAP)
        two = self.two
        self.three = send(two, Z1)
        self.four = send(jnp.concatenate([self.mine(two), two[2 * UNIT :]], axis=0), Z2)
        self.other_three, self.other_four = send(self.three, SWAP), send(self.four, SWAP)

    def near(self):
        return [*map(self.mine, (self.one, self.other_one, self.two, self.other_two))]

    def far(self):
        return [self.mine(self.three), self.mine(self.other_three), self.four[:UNIT]]

    def direct(self):
        return [
            self.one,
            self.other_one,
            self.two,
            self.other_two,
            self.three,
            self.other_three,
            self.four,
            self.other_four,
        ]


def round_once(chunk):
    return send(chunk, RING_UP), send(chunk, RING_DOWN)


def round_twice(up, down):
    cut = (up.shape[0] + 1) // 2
    return send(up[:cut], RING_UP), send(down[cut:], RING_DOWN)


def swapped(values):
    return tuple(send(v, SWAP) for v in values)


def start_copies(where, whole, sems):
    z, sign = where[8], where[9]
    copies = []

    def at(offset):
        return lax.rem(z + offset + 2 * NZ, NZ)

    def fetch(src, dst):
        copy = pltpu.make_async_copy(src, dst, sems.at[len(copies)])
        copy.start()
        copies.append(copy)
        return copy

    def fetch_unit(src, start, tap, spot):
        piece = pl.ds(pl.multiple_of((tap - 1) * PIECE, PIECE), PIECE)
        return [
            fetch(src.at[pl.ds(start, SLAB)], whole.at[tap, spot]),
            fetch(src.at[pl.ds(start + SLAB, PIECE)], whole.at[0, spot, piece]),
        ]

    def fetch_last(src, start, spot):
        return fetch(src.at[pl.ds(start, PIECE)], whole.at[0, spot, pl.ds(8 * PIECE, PIECE)])

    return z, sign, at, fetch, fetch_unit, fetch_last


def join(grown, joined):
    for f in range(6):
        for r in range(5):
            line = grown[f, r].astype(F32)
            column = lax.broadcasted_iota(jnp.int32, line.shape, 0)
            before = jnp.where(column == 0, 0.0, pltpu.roll(line, 1, 0))
            after_ = jnp.where(column == 47, 0.0, pltpu.roll(line, 47, 0))
            joined[f, r, :, :C] = before.astype(BF)
            joined[f, r, :, C : 2 * C] = grown[f, r]
            joined[f, r, :, 2 * C :] = after_.astype(BF)


def product(joined, whole, tap):
    window = joined[pl.ds(lax.div(tap, 3), 4), pl.ds(lax.rem(tap, 3), 3)]
    return jnp.dot(
        window.reshape(576, 3 * C), whole[tap].reshape(NZ * SLAB, C), preferred_element_type=F32
    )


def ring_offsets(turn, split):
    near, far = [turn, -turn, 2 * turn, -2 * turn], [3 * turn, -3 * turn, 4]
    return [near, far] if split else [near + far]


def early_kernel(split, where, grown, slab, *refs):
    n = 8 + 4 * (2 if split else 1)
    arrays, (total, tap0, joined, whole, sems) = refs[:n], refs[n:]
    z, sign, at, fetch, fetch_unit, fetch_last = start_copies(where, whole, sems)
    tap = [where[k] for k in range(8)]
    needs = {k: [] for k in ("slab", "own", "last", 2, 3, 5, 6)}
    needs["slab"].append(fetch(slab, whole.at[:, z]))
    for step in (1, 2, 3):
        for ref, spot in (
            (arrays[2 * step - 2], at(sign * step)),
            (arrays[2 * step - 1], at(-sign * step)),
        ):
            for k in range(2):
                needs["own"] += fetch_unit(ref, k * UNIT, where[10 + k], spot)
            needs["last"].append(fetch_last(ref, 2 * UNIT, spot))
    needs["own"] += fetch_unit(arrays[6], 0, tap[0], at(4))
    needs["own"] += fetch_unit(arrays[7], 0, tap[1], at(4))
    needs["last"].append(fetch_last(arrays[6], UNIT, at(4)))
    rest = arrays[8:]
    count = 2 if split else 1
    for base, turn, group in ((2, sign, rest[: 2 * count]), (5, -sign, rest[2 * count :])):
        for part, offsets in enumerate(ring_offsets(turn, split)):
            for k, offset in enumerate(offsets):
                for way in range(2):
                    needs[base + way] += fetch_unit(
                        group[2 * part + way].at[k], 0, tap[base + way], at(offset)
                    )
    join(grown, joined)
    for key in ("slab", "own"):
        for copy in needs[key]:
            copy.wait()
    total[...] = product(joined, whole, where[10])
    total[...] += product(joined, whole, where[11])
    for key in (2, 5, 3, 6):
        for copy in needs[key]:
            copy.wait()
        total[...] += product(joined, whole, tap[key])
    for copy in needs["last"]:
        copy.wait()
    tap0[...] = whole[0]


def late_kernel(second, split, where, total, tap0, joined, slab, *refs):
    n = 4 * (2 if split else 1)
    arrays, (extra, gain, bias, out, whole, sems) = refs[:n], refs[n:]
    z, sign, at, fetch, fetch_unit, fetch_last = start_copies(where, whole, sems)
    tap = [where[k] for k in range(8)]
    needs = {4: [], 7: []}
    start = fetch(tap0, whole.at[0])
    own = [fetch(slab.at[tap[k]], whole.at[tap[k], z]) for k in (4, 7)]
    start.wait()
    count = 2 if split else 1
    for base, turn, group in ((4, sign, arrays[: 2 * count]), (7, -sign, arrays[2 * count :])):
        for part, offsets in enumerate(ring_offsets(turn, split)):
            cut = (len(offsets) + 1) // 2
            for k, offset in enumerate(offsets):
                src = group[2 * part].at[k] if k < cut else group[2 * part + 1].at[k - cut]
                needs[base] += fetch_unit(src, 0, tap[base], at(offset))
    result = total[...]
    for copy in own + needs[4]:
        copy.wait()
    result += product(joined, whole, tap[4])
    for copy in needs[7]:
        copy.wait()
    result += product(joined, whole, tap[7])
    result += product(joined, whole, 0)
    hidden = result + bias[...]
    if second:
        result = hidden + extra[...].astype(F32)
    else:
        result = activate(hidden, gain[...])
    out[...] = result.astype(BF)


ANY = pl.BlockSpec(memory_space=pl.ANY)
VMEM = pl.BlockSpec(memory_space=pltpu.VMEM)
SMEM = pl.BlockSpec(memory_space=pltpu.SMEM)


def cost(taps):
    return pl.CostEstimate(
        flops=2 * 576 * taps * 3 * C * C, bytes_accessed=taps * 3 * C * C * 2, transcendentals=0
    )


def conv_early(grown, slab, arrays, where, split, name):
    return pl.pallas_call(
        functools.partial(early_kernel, split),
        out_shape=[
            jax.ShapeDtypeStruct((576, C), F32),
            jax.ShapeDtypeStruct((NZ, SLAB, C), BF),
            jax.ShapeDtypeStruct((6, 5, 48, 3 * C), BF),
        ],
        in_specs=[SMEM, VMEM, ANY, *[ANY] * len(arrays)],
        out_specs=[VMEM, VMEM, VMEM],
        scratch_shapes=[pltpu.VMEM((9, NZ, SLAB, C), BF), pltpu.SemaphoreType.DMA((100,))],
        compiler_params=pltpu.CompilerParams(vmem_limit_bytes=24 * 2**20),
        cost_estimate=cost(6),
        name=name,
    )(where, grown, slab, *arrays)


def conv_late(early, slab, arrays, extra, gain, bias, where, split, second, name):
    out = pl.pallas_call(
        functools.partial(late_kernel, second, split),
        out_shape=jax.ShapeDtypeStruct((576, C), BF),
        in_specs=[SMEM, VMEM, ANY, VMEM, ANY, *[ANY] * len(arrays), VMEM, VMEM, VMEM],
        out_specs=VMEM,
        scratch_shapes=[pltpu.VMEM((9, NZ, SLAB, C), BF), pltpu.SemaphoreType.DMA((40,))],
        compiler_params=pltpu.CompilerParams(vmem_limit_bytes=24 * 2**20),
        cost_estimate=cost(3),
        name=name,
    )(where, *early, slab, *arrays, extra, gain, bias)
    return out.reshape(4, 3, 48, C)


def local(latent, gain_first, weight_first, bias_first, gain_second, weight_second, bias_second):
    y, x, z, core = (lax.axis_index(name) for name in AXES)
    tap_x, tap_y = 1 + x, 5 + y

    def taps(step):
        across, down = 1 + lax.rem(x + step + NX, NX), 5 + lax.rem(y + step + NY, NY)
        return jnp.where(core == 0, across, down), jnp.where(core == 0, down, across)

    mine, other = zip(*(taps(step) for step in (0, -1, 1, 2)))
    where = jnp.stack(
        [mine[0], other[0], *mine[1:], *other[1:], z, jnp.where(core == 0, -1, 1), tap_x, tap_y]
    ).astype(jnp.int32)
    row = lambda v: v.reshape(1, C)
    flat = latent.reshape(576, C)

    one = Gather(weight_first.reshape(9, 72, C), core, tap_x, tap_y)
    both = one.start()
    one.hop(both)
    first = activate(after(latent, both), gain_first).astype(BF)
    grown = grow(first)

    near = round_once(jnp.stack(one.near()))
    far = round_once(jnp.stack(one.far()))
    near_two, far_two = round_twice(*near), round_twice(*far)
    arrays = [*one.direct(), *near, *far, *swapped(near), *swapped(far)]
    early = conv_early(grown, one.slab, arrays, where, True, "first_early")
    arrays = [*near_two, *far_two, *swapped(near_two), *swapped(far_two)]

    two = Gather(after(weight_second, both).reshape(9, 72, C), core, tap_x, tap_y)
    two.hop(after(two.start(), one.three, one.four))
    ring = round_once(after(jnp.stack(two.near() + two.far()), *far))
    ring_two = round_twice(*ring)

    second = conv_late(
        early, one.slab, arrays, flat, row(gain_second), row(bias_first), where, True, False, "first_late"
    )
    grown = grow(second)
    arrays = [*two.direct(), *ring, *swapped(ring)]
    early = conv_early(grown, two.slab, arrays, where, False, "second_early")
    arrays = [*ring_two, *swapped(ring_two)]
    return conv_late(
        early, two.slab, arrays, flat, row(gain_second), row(bias_second), where, False, True, "second_late"
    )


def solution(mesh):
    fine = Mesh(mesh.devices.reshape(NY, NX, NZ, 2), AXES)
    frames = P(("z", "c"), ("y", "x"), None, None)
    slices = P(None, None, ("z", "c"), None)
    return jax.shard_map(
        local,
        mesh=fine,
        in_specs=(frames, P(), slices, P(), P(), slices, P()),
        out_specs=frames,
        check_vma=False,
    )
```

```python
import functools

import jax
import jax.numpy as jnp
from jax import lax
from jax.experimental import pallas as pl
from jax.experimental.pallas import tpu as pltpu
from jax.sharding import Mesh
from jax.sharding import PartitionSpec as P

BF = jnp.bfloat16
F32 = jnp.float32
C = 384
NY, NX, NZ = 4, 4, 8
AXES = ("y", "x", "z", "c")
SLAB = 144
PIECE = 16
UNIT = SLAB + PIECE


def index(y, x, z, c):
    return ((y % NY * NX + x % NX) * NZ + z % NZ) * 2 + c


def perm(to):
    return [
        (index(y, x, z, c), index(*to(y, x, z, c)))
        for y in range(NY)
        for x in range(NX)
        for z in range(NZ)
        for c in range(2)
    ]


def along_z(steps):
    return perm(lambda y, x, z, c: (y, x, z + steps if c == 0 else z - steps, c))


Z1, Z2 = along_z(1), along_z(2)
SWAP = perm(lambda y, x, z, c: (y, x, z, 1 - c))
RING_UP = perm(lambda y, x, z, c: (y, x + 1, z, c) if c == 0 else (y + 1, x, z, c))
RING_DOWN = perm(lambda y, x, z, c: (y, x - 1, z, c) if c == 0 else (y - 1, x, z, c))


def neighbours(tile_step, group_step):
    tiles, groups = NY * NX, NZ * 2
    return [
        (t * groups + g, (t + tile_step) * groups + g + group_step)
        for t in range(tiles)
        for g in range(groups)
        if 0 <= t + tile_step < tiles and 0 <= g + group_step < groups
    ]


def send(value, pairs):
    return lax.ppermute(value, AXES, pairs)


def activate(values, gain):
    wide = values.astype(F32)
    scaled = wide * lax.rsqrt(jnp.mean(wide * wide, axis=-1, keepdims=True) + 1e-06) * gain
    return jax.nn.silu(scaled)


def after(value, *others):
    return lax.optimization_barrier((value, others))[0]


def grow(own):
    tail = own[2:]
    above = send(own[:, 1:], neighbours(1, 0))
    below = send(own[:, :2], neighbours(-1, 0))
    earlier = send(tail, neighbours(0, 1))
    corner_above = send(tail[:, 1:], neighbours(1, 1))
    corner_below = send(tail[:, :2], neighbours(-1, 1))
    return [
        jnp.concatenate([corner_above, earlier, corner_below], axis=1),
        jnp.concatenate([above[:2], own[:2], below[:2]], axis=1),
        jnp.concatenate([above[2:], own[2:], below[2:]], axis=1),
    ]


def gather(weight, z, core, tap_x, tap_y):
    first_core = core == 0
    local_taps = [lax.dynamic_slice_in_dim(weight, tap, 1, axis=0)[0] for tap in (tap_x, tap_y)]
    own = jnp.stack([*local_taps, weight[0]])
    other = send(own, SWAP)
    slab = jnp.concatenate(
        [jnp.where(first_core, own, other), jnp.where(first_core, other, own)], axis=1
    )
    piece = [
        lax.dynamic_slice_in_dim(slab[2], (tap - 1) * PIECE, PIECE, axis=0) for tap in (tap_x, tap_y)
    ]
    both = jnp.concatenate([slab[0], piece[0], slab[1], piece[1], slab[2, 8 * PIECE :]], axis=0)

    def mine(value):
        return jnp.where(first_core, value[:UNIT], value[UNIT : 2 * UNIT])

    one, two = send(both, Z1), send(both, Z2)
    three = send(two, Z1)
    four = send(jnp.concatenate([mine(two), two[2 * UNIT :]], axis=0), Z2)
    sent = [one, two, three]
    other = [send(v, SWAP) for v in sent]
    plus = [jnp.where(first_core, o, s) for s, o in zip(sent, other)]
    minus = [jnp.where(first_core, s, o) for s, o in zip(sent, other)]
    turn = lax.rem(NZ - z, NZ)

    def in_order(pick, four):
        parts = [pick(both), *map(pick, plus), four, *map(pick, minus[::-1])]
        return lax.dynamic_slice_in_dim(jnp.stack(parts + parts), turn, NZ, axis=0)

    last = in_order(lambda v: v[2 * UNIT :], four[UNIT:])
    chunk = in_order(mine, four[:UNIT])
    up, down = send(chunk, RING_UP), send(chunk, RING_DOWN)
    far_up, far_down = send(up[: NZ // 2], RING_UP), send(down[NZ // 2 :], RING_DOWN)
    pieces = [chunk, up, down, far_up, far_down]
    return [*pieces, *(send(v, SWAP) for v in pieces), last], both


def assemble_kernel(where, *refs):
    *arrays, last, whole, sems = refs
    copies = []

    def fetch(src, dst):
        copy = pltpu.make_async_copy(src, dst, sems.at[len(copies)])
        copy.start()
        copies.append(copy)

    half = NZ // 2
    for k, src in enumerate(arrays):
        tap = where[k - k // 5 - k % 5 // 4]
        slabs = {3: pl.ds(0, half), 4: pl.ds(half, half)}.get(k % 5, pl.ds(0, NZ))
        piece = pl.ds(pl.multiple_of((tap - 1) * PIECE, PIECE), PIECE)
        fetch(src.at[:, pl.ds(0, SLAB)], whole.at[tap, slabs])
        fetch(src.at[:, pl.ds(SLAB, PIECE)], whole.at[0, slabs, piece])
    fetch(last, whole.at[0, :, pl.ds(8 * PIECE, PIECE)])
    for copy in copies:
        copy.wait()


ANY = pl.BlockSpec(memory_space=pl.ANY)
VMEM = pl.BlockSpec(memory_space=pltpu.VMEM)
SMEM = pl.BlockSpec(memory_space=pltpu.SMEM)


def assemble(arrays, where):
    whole = pl.pallas_call(
        assemble_kernel,
        out_shape=jax.ShapeDtypeStruct((9, NZ, SLAB, C), BF),
        in_specs=[SMEM, *[ANY] * len(arrays)],
        out_specs=VMEM,
        scratch_shapes=[pltpu.SemaphoreType.DMA((2 * len(arrays) - 1,))],
        compiler_params=pltpu.CompilerParams(vmem_limit_bytes=12 * 2**20),
        name="assemble",
    )(where, *arrays)
    return whole.reshape(9, 3 * C, C)


def convolve(frames, rows, whole, wide):
    size = 2 * rows * 48
    for t in range(3):
        left = jnp.concatenate(
            [
                jnp.concatenate(
                    [frames[f][k : k + rows].reshape(rows * 48, C) for f in (t, t + 1)], axis=0
                )
                for k in range(3)
            ],
            axis=1,
        )
        right = jnp.concatenate(
            [
                jnp.concatenate([whole(3 * t + k)[d * C : (d + 1) * C] for d in range(3)], axis=1)
                for k in range(3)
            ],
            axis=0,
        )
        part = jnp.dot(left, right, preferred_element_type=F32)
        if t == 0:
            wide[...] = part
        else:
            wide[...] += part
    column = lax.broadcasted_iota(jnp.int32, (48, C), 0)
    lines = []
    for i in range(2 * rows):
        line = wide[48 * i : 48 * i + 48]
        before = jnp.where(column == 0, 0.0, pltpu.roll(line[:, :C], 1, 0))
        behind = jnp.where(column == 47, 0.0, pltpu.roll(line[:, 2 * C :], 47, 0))
        lines.append(before + line[:, C : 2 * C] + behind)
    return lines


def first_kernel(tile, low, high, weight, bias, gain, out, wide):
    frames = [low[0], low[1], high[0], high[1]]
    lines = convolve(frames, 5, lambda tap: weight[tap], wide)
    for i, line in enumerate(lines):
        result = activate(line + bias[...], gain[...])
        if i % 5 == 0:
            result = jnp.where(tile[0] == 0, 0.0, result)
        if i % 5 == 4:
            result = jnp.where(tile[0] == NY * NX - 1, 0.0, result)
        out[i // 5, i % 5] = result.astype(BF)


def conv_first(low, high, weight, bias, gain, tile):
    return pl.pallas_call(
        first_kernel,
        out_shape=jax.ShapeDtypeStruct((2, 5, 48, C), BF),
        in_specs=[SMEM] + [VMEM] * 5,
        out_specs=VMEM,
        scratch_shapes=[pltpu.VMEM((480, 3 * C), F32)],
        compiler_params=pltpu.CompilerParams(vmem_limit_bytes=20 * 2**20),
        cost_estimate=cost(480),
        name="conv_first",
    )(tile, low, high, weight, bias, gain)


def second_kernel(start, low, high, weight, latent, bias, *refs):
    out, wide, done, sem = refs[-4:]
    frames = [low[0], low[1], high[0], high[1]]
    lines = convolve(frames, 3, lambda tap: weight[tap], wide)
    for i, line in enumerate(lines):
        at = start + 48 * i
        done[48 * i : 48 * i + 48] = (
            line + bias[...] + latent[at : at + 48].astype(F32)
        ).astype(BF)
    copy = pltpu.make_async_copy(done, out.at[pl.ds(start, 288)], sem)
    copy.start()
    copy.wait()


def conv_second(low, high, weight, latent, bias, partial):
    start = 288 if partial is None else 0
    return pl.pallas_call(
        functools.partial(second_kernel, start),
        out_shape=jax.ShapeDtypeStruct((576, C), BF),
        in_specs=[VMEM] * 5 + ([] if partial is None else [ANY]),
        out_specs=ANY,
        input_output_aliases={} if partial is None else {5: 0},
        scratch_shapes=[
            pltpu.VMEM((288, 3 * C), F32),
            pltpu.VMEM((288, C), BF),
            pltpu.SemaphoreType.DMA,
        ],
        compiler_params=pltpu.CompilerParams(vmem_limit_bytes=20 * 2**20),
        cost_estimate=cost(288),
        name="second_late" if start else "second_early",
    )(low, high, weight, latent, bias, *([] if partial is None else [partial]))


def cost(size):
    return pl.CostEstimate(
        flops=2 * size * 27 * C * C, bytes_accessed=27 * C * C * 2, transcendentals=0
    )


def local(latent, gain_first, weight_first, bias_first, gain_second, weight_second, bias_second):
    y, x, z, core = (lax.axis_index(name) for name in AXES)
    tap_x, tap_y = 1 + x, 5 + y

    def taps(step):
        across, down = 1 + lax.rem(x + step + NX, NX), 5 + lax.rem(y + step + NY, NY)
        return jnp.where(core == 0, across, down), jnp.where(core == 0, down, across)

    mine, other = zip(*(taps(step) for step in (0, -1, 1, 2)))
    where = jnp.stack([*mine, *other]).astype(jnp.int32)
    tile = (y * NX + x).astype(jnp.int32).reshape(1)
    row = lambda v: v.reshape(1, C)

    whole_first = lax.all_gather(weight_first, ("z", "c"), axis=2, tiled=True)
    pieces, both = gather(weight_second.reshape(9, 72, C), z, core, tap_x, tap_y)
    first = activate(after(latent, both), gain_first).astype(BF)
    earlier, low, high = grow(first)
    whole_second = assemble(pieces, where)

    scales = row(bias_first), row(gain_second), tile
    whole_first = whole_first.reshape(9, 3 * C, C)
    second_high = conv_first(low, high, whole_first, *scales)
    second_earlier = send(second_high, neighbours(0, 1))
    second_low = conv_first(earlier, low, whole_first, *scales)
    rest = whole_second, latent.reshape(576, C), row(bias_second)
    partial = conv_second(second_low, second_high, *rest, None)
    return conv_second(second_earlier, second_low, *rest, partial).reshape(4, 3, 48, C)


def solution(mesh):
    fine = Mesh(mesh.devices.reshape(NY, NX, NZ, 2), AXES)
    frames = P(("z", "c"), ("y", "x"), None, None)
    slices = P(None, None, ("z", "c"), None)
    return jax.shard_map(
        local,
        mesh=fine,
        in_specs=(frames, P(), slices, P(), P(), slices, P()),
        out_specs=frames,
        check_vma=False,
    )
```

```python
import functools

import jax
import jax.numpy as jnp
from jax import lax
from jax.experimental import pallas as pl
from jax.experimental.pallas import tpu as pltpu
from jax.sharding import Mesh
from jax.sharding import PartitionSpec as P

BF = jnp.bfloat16
F32 = jnp.float32
C = 384
NY, NX, NZ = 4, 4, 8
AXES = ("y", "x", "z", "c")
SLAB = 144
PART = 40
BLOCK = 160


def index(y, x, z, c):
    return ((y % NY * NX + x % NX) * NZ + z % NZ) * 2 + c


def perm(to):
    return [
        (index(y, x, z, c), index(*to(y, x, z, c)))
        for y in range(NY)
        for x in range(NX)
        for z in range(NZ)
        for c in range(2)
    ]


def along_z(steps):
    return perm(lambda y, x, z, c: (y, x, z + steps if c == 0 else z - steps, c))


Z1, Z2 = along_z(1), along_z(2)
SWAP = perm(lambda y, x, z, c: (y, x, z, 1 - c))
RING_UP = perm(lambda y, x, z, c: (y, x + 1, z, c) if c == 0 else (y + 1, x, z, c))
RING_DOWN = perm(lambda y, x, z, c: (y, x - 1, z, c) if c == 0 else (y - 1, x, z, c))

CROSS_UP = perm(lambda y, x, z, c: (y + 1, x, z, c) if c == 0 else (y, x + 1, z, c))
CROSS_DOWN = perm(lambda y, x, z, c: (y - 1, x, z, c) if c == 0 else (y, x - 1, z, c))


def neighbours(tile_step, group_step):
    tiles, groups = NY * NX, NZ * 2
    return [
        (t * groups + g, (t + tile_step) * groups + g + group_step)
        for t in range(tiles)
        for g in range(groups)
        if 0 <= t + tile_step < tiles and 0 <= g + group_step < groups
    ]


def send(value, pairs):
    return lax.ppermute(value, AXES, pairs)


def activate(values, gain):
    wide = values.astype(F32)
    scaled = wide * lax.rsqrt(jnp.mean(wide * wide, axis=-1, keepdims=True) + 1e-06) * gain
    return jax.nn.silu(scaled)


def after(value, *others):
    return lax.optimization_barrier((value, others))[0]


def grow(own):
    tail = own[2:]
    above = send(own[:, 1:], neighbours(1, 0))
    below = send(own[:, :2], neighbours(-1, 0))
    earlier = send(tail, neighbours(0, 1))
    corner_above = send(tail[:, 1:], neighbours(1, 1))
    corner_below = send(tail[:, :2], neighbours(-1, 1))
    return [
        jnp.concatenate([corner_above, earlier, corner_below], axis=1),
        jnp.concatenate([above[:2], own[:2], below[:2]], axis=1),
        jnp.concatenate([above[2:], own[2:], below[2:]], axis=1),
    ]


def gather(weight, y, x, z, core):
    first_core = core == 0
    other = send(weight, SWAP)
    slab = jnp.concatenate(
        [jnp.where(first_core, weight, other), jnp.where(first_core, other, weight)], axis=1
    ).reshape(9 * SLAB, C)
    starts = BLOCK * 2 * y + PART * x, BLOCK * 2 * x + BLOCK + PART * y
    both = jnp.concatenate(
        [*(lax.dynamic_slice_in_dim(slab, at, PART, axis=0) for at in starts), slab[8 * BLOCK :]],
        axis=0,
    )
    one, two = send(both, Z1), send(both, Z2)
    three, four = send(two, Z1), send(two, Z2)
    sent = jnp.stack([one, two, three])
    other = send(sent, SWAP)
    plus, minus = jnp.where(first_core, other, sent), jnp.where(first_core, sent, other)
    parts = [both, plus[0], plus[1], plus[2], four, minus[2], minus[1], minus[0]]
    slabs = lax.dynamic_slice_in_dim(jnp.stack(parts + parts), lax.rem(NZ - z, NZ), NZ, axis=0)
    last = slabs[:, 2 * PART :]
    chunk = jnp.where(first_core, slabs[:, :PART], slabs[:, PART : 2 * PART])

    def ring(chunk, up_pairs, down_pairs):
        half = NZ // 2
        up, down = send(chunk, up_pairs), send(chunk, down_pairs)
        return up, down, send(up[:half], up_pairs), send(down[half:], down_pairs)

    up, down, far_up, far_down = ring(chunk, RING_UP, RING_DOWN)
    parts = [chunk, down, jnp.concatenate([far_up, far_down], axis=0), up]
    spot = lax.rem(4 - jnp.where(first_core, x, y), 4)
    turned = lax.dynamic_slice_in_dim(jnp.stack(parts + parts), spot, 4, axis=0)
    chunk = turned.transpose(1, 0, 2, 3).reshape(NZ, BLOCK, C)
    pieces = [chunk, *ring(chunk, CROSS_UP, CROSS_DOWN)]
    return [*pieces, *(send(v, SWAP) for v in pieces), last], chunk


def assemble_kernel(where, *refs):
    *arrays, last, whole, sems = refs
    copies = []

    def fetch(src, dst):
        copy = pltpu.make_async_copy(src, dst, sems.at[len(copies)])
        copy.start()
        copies.append(copy)

    half = NZ // 2
    for k, src in enumerate(arrays):
        at = pl.multiple_of(where[k - k // 5 - k % 5 // 4], BLOCK)
        slabs = {3: pl.ds(0, half), 4: pl.ds(half, half)}.get(k % 5, pl.ds(0, NZ))
        fetch(src, whole.at[slabs, pl.ds(at, BLOCK)])
    fetch(last, whole.at[:, pl.ds(8 * BLOCK, 9 * SLAB - 8 * BLOCK)])
    for copy in copies:
        copy.wait()


ANY = pl.BlockSpec(memory_space=pl.ANY)
VMEM = pl.BlockSpec(memory_space=pltpu.VMEM)
SMEM = pl.BlockSpec(memory_space=pltpu.SMEM)


def assemble(arrays, where):
    return pl.pallas_call(
        assemble_kernel,
        out_shape=jax.ShapeDtypeStruct((NZ, 9 * SLAB, C), BF),
        in_specs=[SMEM, *[ANY] * len(arrays)],
        out_specs=VMEM,
        scratch_shapes=[pltpu.SemaphoreType.DMA((len(arrays),))],
        compiler_params=pltpu.CompilerParams(vmem_limit_bytes=12 * 2**20),
        name="assemble",
    )(where, *arrays)


def convolve(frames, rows, whole, wide):
    size = 2 * rows * 48
    for t in range(3):
        left = jnp.concatenate(
            [
                jnp.concatenate(
                    [frames[f][k : k + rows].reshape(rows * 48, C) for f in (t, t + 1)], axis=0
                )
                for k in range(3)
            ],
            axis=1,
        )
        right = jnp.concatenate(
            [
                jnp.concatenate([whole(3 * t + k)[d * C : (d + 1) * C] for d in range(3)], axis=1)
                for k in range(3)
            ],
            axis=0,
        )
        part = jnp.dot(left, right, preferred_element_type=F32)
        if t == 0:
            wide[...] = part
        else:
            wide[...] += part
    column = lax.broadcasted_iota(jnp.int32, (48, C), 0)
    lines = []
    for i in range(2 * rows):
        line = wide[48 * i : 48 * i + 48]
        before = jnp.where(column == 0, 0.0, pltpu.roll(line[:, :C], 1, 0))
        behind = jnp.where(column == 47, 0.0, pltpu.roll(line[:, 2 * C :], 47, 0))
        lines.append(before + line[:, C : 2 * C] + behind)
    return lines


def first_kernel(tile, low, high, weight, bias, gain, out, wide):
    frames = [low[0], low[1], high[0], high[1]]
    lines = convolve(frames, 5, lambda tap: weight[tap], wide)
    for i, line in enumerate(lines):
        result = activate(line + bias[...], gain[...])
        if i % 5 == 0:
            result = jnp.where(tile[0] == 0, 0.0, result)
        if i % 5 == 4:
            result = jnp.where(tile[0] == NY * NX - 1, 0.0, result)
        out[i // 5, i % 5] = result.astype(BF)


def conv_first(low, high, weight, bias, gain, tile):
    return pl.pallas_call(
        first_kernel,
        out_shape=jax.ShapeDtypeStruct((2, 5, 48, C), BF),
        in_specs=[SMEM] + [VMEM] * 5,
        out_specs=VMEM,
        scratch_shapes=[pltpu.VMEM((480, 3 * C), F32)],
        compiler_params=pltpu.CompilerParams(vmem_limit_bytes=12 * 2**20),
        cost_estimate=cost(480),
        name="conv_first",
    )(tile, low, high, weight, bias, gain)


def slab_rows(weight, tap):
    return weight[:, SLAB * tap : SLAB * (tap + 1)].reshape(3 * C, C)


def second_kernel(start, low, high, weight, latent, bias, *refs):
    out, wide, done, sem = refs[-4:]
    frames = [low[0], low[1], high[0], high[1]]
    lines = convolve(frames, 3, lambda tap: slab_rows(weight, tap), wide)
    for i, line in enumerate(lines):
        at = start + 48 * i
        done[48 * i : 48 * i + 48] = (
            line + bias[...] + latent[at : at + 48].astype(F32)
        ).astype(BF)
    copy = pltpu.make_async_copy(done, out.at[pl.ds(start, 288)], sem)
    copy.start()
    copy.wait()


def conv_second(low, high, weight, latent, bias, partial):
    start = 288 if partial is None else 0
    return pl.pallas_call(
        functools.partial(second_kernel, start),
        out_shape=jax.ShapeDtypeStruct((576, C), BF),
        in_specs=[VMEM] * 5 + ([] if partial is None else [ANY]),
        out_specs=ANY,
        input_output_aliases={} if partial is None else {5: 0},
        scratch_shapes=[
            pltpu.VMEM((288, 3 * C), F32),
            pltpu.VMEM((288, C), BF),
            pltpu.SemaphoreType.DMA,
        ],
        compiler_params=pltpu.CompilerParams(vmem_limit_bytes=12 * 2**20),
        cost_estimate=cost(288),
        name="second_late" if start else "second_early",
    )(low, high, weight, latent, bias, *([] if partial is None else [partial]))


def cost(size):
    return pl.CostEstimate(
        flops=2 * size * 27 * C * C, bytes_accessed=27 * C * C * 2, transcendentals=0
    )


def local(latent, gain_first, weight_first, bias_first, gain_second, weight_second, bias_second):
    y, x, z, core = (lax.axis_index(name) for name in AXES)

    def starts(step):
        down, across = lax.rem(y + step + NY, NY), lax.rem(x + step + NX, NX)
        down, across = 2 * BLOCK * down, 2 * BLOCK * across + BLOCK
        return jnp.where(core == 0, down, across), jnp.where(core == 0, across, down)

    mine, other = zip(*(starts(step) for step in (0, -1, 1, 2)))
    where = jnp.stack([*mine, *other]).astype(jnp.int32)
    tile = (y * NX + x).astype(jnp.int32).reshape(1)
    row = lambda v: v.reshape(1, C)

    whole_first = lax.all_gather(weight_first, ("z", "c"), axis=2, tiled=True)
    pieces, chunk = gather(weight_second.reshape(9, 72, C), y, x, z, core)
    first = activate(after(latent, chunk), gain_first).astype(BF)
    earlier, low, high = grow(first)

    scales = row(bias_first), row(gain_second), tile
    whole_first = whole_first.reshape(9, 3 * C, C)
    second_high = conv_first(low, high, whole_first, *scales)
    second_earlier = send(second_high, neighbours(0, 1))
    second_low = conv_first(earlier, low, whole_first, *scales)
    whole_second = assemble(after(pieces, second_low), where)
    rest = whole_second, latent.reshape(576, C), row(bias_second)
    partial = conv_second(second_low, second_high, *rest, None)
    return conv_second(second_earlier, second_low, *rest, partial).reshape(4, 3, 48, C)


def solution(mesh):
    fine = Mesh(mesh.devices.reshape(NY, NX, NZ, 2), AXES)
    frames = P(("z", "c"), ("y", "x"), None, None)
    slices = P(None, None, ("z", "c"), None)
    return jax.shard_map(
        local,
        mesh=fine,
        in_specs=(frames, P(), slices, P(), P(), slices, P()),
        out_specs=frames,
        check_vma=False,
    )
```

```python
import functools

import jax
import jax.numpy as jnp
from jax import lax
from jax.experimental import pallas as pl
from jax.experimental.pallas import tpu as pltpu
from jax.sharding import Mesh
from jax.sharding import PartitionSpec as P

BF = jnp.bfloat16
F32 = jnp.float32
C = 384
NY, NX, NZ = 4, 4, 8
AXES = ("y", "x", "z", "c")
SLAB = 144
PART = 40
BLOCK = 160


def index(y, x, z, c):
    return ((y % NY * NX + x % NX) * NZ + z % NZ) * 2 + c


def perm(to):
    return [
        (index(y, x, z, c), index(*to(y, x, z, c)))
        for y in range(NY)
        for x in range(NX)
        for z in range(NZ)
        for c in range(2)
    ]


def along_z(steps):
    return perm(lambda y, x, z, c: (y, x, z + steps if c == 0 else z - steps, c))


Z1, Z2 = along_z(1), along_z(2)
SWAP = perm(lambda y, x, z, c: (y, x, z, 1 - c))
RING_UP = perm(lambda y, x, z, c: (y, x + 1, z, c) if c == 0 else (y + 1, x, z, c))
RING_DOWN = perm(lambda y, x, z, c: (y, x - 1, z, c) if c == 0 else (y - 1, x, z, c))

CROSS_UP = perm(lambda y, x, z, c: (y + 1, x, z, c) if c == 0 else (y, x + 1, z, c))
CROSS_DOWN = perm(lambda y, x, z, c: (y - 1, x, z, c) if c == 0 else (y, x - 1, z, c))


def neighbours(tile_step, group_step):
    tiles, groups = NY * NX, NZ * 2
    return [
        (t * groups + g, (t + tile_step) * groups + g + group_step)
        for t in range(tiles)
        for g in range(groups)
        if 0 <= t + tile_step < tiles and 0 <= g + group_step < groups
    ]


def send(value, pairs):
    return lax.ppermute(value, AXES, pairs)


def activate(values, gain):
    wide = values.astype(F32)
    scaled = wide * lax.rsqrt(jnp.mean(wide * wide, axis=-1, keepdims=True) + 1e-06) * gain
    return jax.nn.silu(scaled)


def after(value, *others):
    return lax.optimization_barrier((value, others))[0]


def grow_rows(own):
    above = send(own[:, 1:], neighbours(1, 0))
    below = send(own[:, :2], neighbours(-1, 0))
    return jnp.concatenate([above, own, below], axis=1)


def gather(weight, y, x, z, core, rows):
    first_core = core == 0
    other = send(weight, SWAP)
    slab = jnp.concatenate(
        [jnp.where(first_core, weight, other), jnp.where(first_core, other, weight)], axis=1
    ).reshape(9 * SLAB, C)
    starts = BLOCK * 2 * y + PART * x, BLOCK * 2 * x + BLOCK + PART * y
    both = jnp.concatenate(
        [*(lax.dynamic_slice_in_dim(slab, at, PART, axis=0) for at in starts), slab[8 * BLOCK :]],
        axis=0,
    )
    one, two = send(both, Z1), send(both, Z2)
    two = after(two, rows)
    three, four = send(two, Z1), send(two, Z2)
    sent = jnp.stack([one, two, three])
    other = send(sent, SWAP)
    plus, minus = jnp.where(first_core, other, sent), jnp.where(first_core, sent, other)
    parts = [both, plus[0], plus[1], plus[2], four, minus[2], minus[1], minus[0]]
    slabs = lax.dynamic_slice_in_dim(jnp.stack(parts + parts), lax.rem(NZ - z, NZ), NZ, axis=0)
    last = slabs[:, 2 * PART :]
    chunk = jnp.where(first_core, slabs[:, :PART], slabs[:, PART : 2 * PART])

    def ring(chunk, up_pairs, down_pairs):
        half = NZ // 2
        up, down = send(chunk, up_pairs), send(chunk, down_pairs)
        return up, down, send(up[:half], up_pairs), send(down[half:], down_pairs)

    up, down, far_up, far_down = ring(chunk, RING_UP, RING_DOWN)
    parts = [chunk, down, jnp.concatenate([far_up, far_down], axis=0), up]
    spot = lax.rem(4 - jnp.where(first_core, x, y), 4)
    turned = lax.dynamic_slice_in_dim(jnp.stack(parts + parts), spot, 4, axis=0)
    chunk = turned.transpose(1, 0, 2, 3).reshape(NZ, BLOCK, C)
    return [chunk, *ring(chunk, CROSS_UP, CROSS_DOWN)], last


def assemble_kernel(where, *refs):
    *arrays, last, whole, sems = refs
    copies = []

    def fetch(src, dst):
        copy = pltpu.make_async_copy(src, dst, sems.at[len(copies)])
        copy.start()
        copies.append(copy)

    half = NZ // 2
    for k, src in enumerate(arrays):
        at = pl.multiple_of(where[k - k // 5 - k % 5 // 4], BLOCK)
        slabs = {3: pl.ds(0, half), 4: pl.ds(half, half)}.get(k % 5, pl.ds(0, NZ))
        fetch(src, whole.at[slabs, pl.ds(at, BLOCK)])
    fetch(last, whole.at[:, pl.ds(8 * BLOCK, 9 * SLAB - 8 * BLOCK)])
    for copy in copies:
        copy.wait()


ANY = pl.BlockSpec(memory_space=pl.ANY)
VMEM = pl.BlockSpec(memory_space=pltpu.VMEM)
SMEM = pl.BlockSpec(memory_space=pltpu.SMEM)


def assemble(arrays, where):
    return pl.pallas_call(
        assemble_kernel,
        out_shape=jax.ShapeDtypeStruct((NZ, 9 * SLAB, C), BF),
        in_specs=[SMEM, *[ANY] * len(arrays)],
        out_specs=VMEM,
        scratch_shapes=[pltpu.SemaphoreType.DMA((len(arrays),))],
        compiler_params=pltpu.CompilerParams(vmem_limit_bytes=12 * 2**20),
        name="assemble",
    )(where, *arrays)


def convolve(frames, rows, whole, wide):
    size = 2 * rows * 48
    for t in range(3):
        left = jnp.concatenate(
            [
                jnp.concatenate(
                    [frames[f][k : k + rows].reshape(rows * 48, C) for f in (t, t + 1)], axis=0
                )
                for k in range(3)
            ],
            axis=1,
        )
        right = jnp.concatenate(
            [
                jnp.concatenate([whole(3 * t + k)[d * C : (d + 1) * C] for d in range(3)], axis=1)
                for k in range(3)
            ],
            axis=0,
        )
        part = jnp.dot(left, right, preferred_element_type=F32)
        if t == 0:
            wide[...] = part
        else:
            wide[...] += part
    column = lax.broadcasted_iota(jnp.int32, (48, C), 0)
    lines = []
    for i in range(2 * rows):
        line = wide[48 * i : 48 * i + 48]
        before = jnp.where(column == 0, 0.0, pltpu.roll(line[:, :C], 1, 0))
        behind = jnp.where(column == 47, 0.0, pltpu.roll(line[:, 2 * C :], 47, 0))
        lines.append(before + line[:, C : 2 * C] + behind)
    return lines


def first_kernel(tile, low, high, weight, bias, gain, out, wide):
    frames = [low[0], low[1], high[0], high[1]]
    lines = convolve(frames, 5, lambda tap: weight[tap], wide)
    for i, line in enumerate(lines):
        result = activate(line + bias[...], gain[...])
        if i % 5 == 0:
            result = jnp.where(tile[0] == 0, 0.0, result)
        if i % 5 == 4:
            result = jnp.where(tile[0] == NY * NX - 1, 0.0, result)
        out[i // 5, i % 5] = result.astype(BF)


def conv_first(low, high, weight, bias, gain, tile):
    return pl.pallas_call(
        first_kernel,
        out_shape=jax.ShapeDtypeStruct((2, 5, 48, C), BF),
        in_specs=[SMEM] + [VMEM] * 5,
        out_specs=VMEM,
        scratch_shapes=[pltpu.VMEM((480, 3 * C), F32)],
        compiler_params=pltpu.CompilerParams(vmem_limit_bytes=12 * 2**20),
        cost_estimate=cost(480),
        name="conv_first",
    )(tile, low, high, weight, bias, gain)


def slab_rows(weight, tap):
    return weight[:, SLAB * tap : SLAB * (tap + 1)].reshape(3 * C, C)


def second_kernel(start, low, high, weight, latent, bias, *refs):
    out, wide, done, sem = refs[-4:]
    frames = [low[0], low[1], high[0], high[1]]
    lines = convolve(frames, 3, lambda tap: slab_rows(weight, tap), wide)
    for i, line in enumerate(lines):
        at = start + 48 * i
        done[48 * i : 48 * i + 48] = (
            line + bias[...] + latent[at : at + 48].astype(F32)
        ).astype(BF)
    copy = pltpu.make_async_copy(done, out.at[pl.ds(start, 288)], sem)
    copy.start()
    copy.wait()


def conv_second(low, high, weight, latent, bias, partial):
    start = 288 if partial is None else 0
    return pl.pallas_call(
        functools.partial(second_kernel, start),
        out_shape=jax.ShapeDtypeStruct((576, C), BF),
        in_specs=[VMEM] * 5 + ([] if partial is None else [ANY]),
        out_specs=ANY,
        input_output_aliases={} if partial is None else {5: 0},
        scratch_shapes=[
            pltpu.VMEM((288, 3 * C), F32),
            pltpu.VMEM((288, C), BF),
            pltpu.SemaphoreType.DMA,
        ],
        compiler_params=pltpu.CompilerParams(vmem_limit_bytes=12 * 2**20),
        cost_estimate=cost(288),
        name="second_late" if start else "second_early",
    )(low, high, weight, latent, bias, *([] if partial is None else [partial]))


def cost(size):
    return pl.CostEstimate(
        flops=2 * size * 27 * C * C, bytes_accessed=27 * C * C * 2, transcendentals=0
    )


def local(latent, gain_first, weight_first, bias_first, gain_second, weight_second, bias_second):
    y, x, z, core = (lax.axis_index(name) for name in AXES)

    def starts(step):
        down, across = lax.rem(y + step + NY, NY), lax.rem(x + step + NX, NX)
        down, across = 2 * BLOCK * down, 2 * BLOCK * across + BLOCK
        return jnp.where(core == 0, down, across), jnp.where(core == 0, across, down)

    mine, other = zip(*(starts(step) for step in (0, -1, 1, 2)))
    where = jnp.stack([*mine, *other]).astype(jnp.int32)
    tile = (y * NX + x).astype(jnp.int32).reshape(1)
    row = lambda v: v.reshape(1, C)

    whole_first = lax.all_gather(weight_first, ("z", "c"), axis=2, tiled=True)
    first = activate(latent, gain_first).astype(BF)
    grown = grow_rows(first)
    low, high = grown[:2], grown[2:]
    pieces, last = gather(weight_second.reshape(9, 72, C), y, x, z, core, grown)
    earlier = send(after(high, pieces[0]), neighbours(0, 1))
    others = [send(v, SWAP) for v in pieces[:3]]

    scales = row(bias_first), row(gain_second), tile
    whole_first = whole_first.reshape(9, 3 * C, C)
    second_high = conv_first(low, high, whole_first, *scales)
    second_earlier = send(second_high, neighbours(0, 1))
    others += [send(v, SWAP) for v in after(pieces[3:], second_high)]
    second_low = conv_first(earlier, low, whole_first, *scales)
    whole_second = assemble(after([*pieces, *others, last], second_low), where)
    rest = whole_second, latent.reshape(576, C), row(bias_second)
    partial = conv_second(second_low, second_high, *rest, None)
    return conv_second(second_earlier, second_low, *rest, partial).reshape(4, 3, 48, C)


def solution(mesh):
    fine = Mesh(mesh.devices.reshape(NY, NX, NZ, 2), AXES)
    frames = P(("z", "c"), ("y", "x"), None, None)
    slices = P(None, None, ("z", "c"), None)
    return jax.shard_map(
        local,
        mesh=fine,
        in_specs=(frames, P(), slices, P(), P(), slices, P()),
        out_specs=frames,
        check_vma=False,
    )
```

```python
import functools

import jax
import jax.numpy as jnp
from jax import lax
from jax.experimental import pallas as pl
from jax.experimental.pallas import tpu as pltpu
from jax.sharding import Mesh
from jax.sharding import PartitionSpec as P

BF = jnp.bfloat16
F32 = jnp.float32
C = 384
NY, NX, NZ = 4, 4, 8
AXES = ("y", "x", "z", "c")
SLAB = 144
PART = 40
BLOCK = 160


def index(y, x, z, c):
    return ((y % NY * NX + x % NX) * NZ + z % NZ) * 2 + c


def perm(to):
    return [
        (index(y, x, z, c), index(*to(y, x, z, c)))
        for y in range(NY)
        for x in range(NX)
        for z in range(NZ)
        for c in range(2)
    ]


def along_z(steps):
    return perm(lambda y, x, z, c: (y, x, z + steps if c == 0 else z - steps, c))


SWAP = perm(lambda y, x, z, c: (y, x, z, 1 - c))
RING_UP = perm(lambda y, x, z, c: (y, x + 1, z, c) if c == 0 else (y + 1, x, z, c))
RING_DOWN = perm(lambda y, x, z, c: (y, x - 1, z, c) if c == 0 else (y - 1, x, z, c))

RING_FAR = perm(lambda y, x, z, c: (y, x + 2, z, c) if c == 0 else (y + 2, x, z, c))
CROSS_UP = perm(lambda y, x, z, c: (y + 1, x, z, c) if c == 0 else (y, x + 1, z, c))
CROSS_DOWN = perm(lambda y, x, z, c: (y - 1, x, z, c) if c == 0 else (y, x - 1, z, c))


def neighbours(tile_step, group_step):
    tiles, groups = NY * NX, NZ * 2
    return [
        (t * groups + g, (t + tile_step) * groups + g + group_step)
        for t in range(tiles)
        for g in range(groups)
        if 0 <= t + tile_step < tiles and 0 <= g + group_step < groups
    ]


def send(value, pairs):
    return lax.ppermute(value, AXES, pairs)


def activate(values, gain):
    wide = values.astype(F32)
    scaled = wide * lax.rsqrt(jnp.mean(wide * wide, axis=-1, keepdims=True) + 1e-06) * gain
    return jax.nn.silu(scaled)


def after(value, *others):
    return lax.optimization_barrier((value, others))[0]


def grow_rows(own):
    above = send(own[:, 1:], neighbours(1, 0))
    below = send(own[:, :2], neighbours(-1, 0))
    return jnp.concatenate([above, own, below], axis=1)


def gather(weight, y, x, z, core, rows):
    first_core = core == 0
    other = send(weight, SWAP)
    slab = jnp.concatenate(
        [jnp.where(first_core, weight, other), jnp.where(first_core, other, weight)], axis=1
    ).reshape(9 * SLAB, C)
    starts = BLOCK * 2 * y + PART * x, BLOCK * 2 * x + BLOCK + PART * y
    both = jnp.concatenate(
        [*(lax.dynamic_slice_in_dim(slab, at, PART, axis=0) for at in starts), slab[8 * BLOCK :]],
        axis=0,
    )
    one, two, three, four = (send(both, along_z(steps)) for steps in (1, 2, 3, 4))
    sent = jnp.stack([one, two, three])
    other = send(sent, SWAP)
    plus, minus = jnp.where(first_core, other, sent), jnp.where(first_core, sent, other)
    parts = [both, plus[0], plus[1], plus[2], four, minus[2], minus[1], minus[0]]
    slabs = lax.dynamic_slice_in_dim(jnp.stack(parts + parts), lax.rem(NZ - z, NZ), NZ, axis=0)
    last = slabs[:, 2 * PART :]
    chunk = jnp.where(first_core, slabs[:, :PART], slabs[:, PART : 2 * PART])

    chunk = after(chunk, rows)
    parts = [chunk, *(send(chunk, pairs) for pairs in (RING_DOWN, RING_FAR, RING_UP))]
    spot = lax.rem(4 - jnp.where(first_core, x, y), 4)
    turned = lax.dynamic_slice_in_dim(jnp.stack(parts + parts), spot, 4, axis=0)
    chunk = turned.transpose(1, 0, 2, 3).reshape(NZ, BLOCK, C)
    half = NZ // 2
    up, down = send(chunk, CROSS_UP), send(chunk, CROSS_DOWN)
    far_up, far_down = send(up[:half], CROSS_UP), send(down[half:], CROSS_DOWN)
    return [chunk, up, down, far_up, far_down], last


def assemble_kernel(where, *refs):
    *arrays, last, whole, sems = refs
    copies = []

    def fetch(src, dst):
        copy = pltpu.make_async_copy(src, dst, sems.at[len(copies)])
        copy.start()
        copies.append(copy)

    half = NZ // 2
    for k, src in enumerate(arrays):
        at = pl.multiple_of(where[k - k // 5 - k % 5 // 4], BLOCK)
        slabs = {3: pl.ds(0, half), 4: pl.ds(half, half)}.get(k % 5, pl.ds(0, NZ))
        fetch(src, whole.at[slabs, pl.ds(at, BLOCK)])
    fetch(last, whole.at[:, pl.ds(8 * BLOCK, 9 * SLAB - 8 * BLOCK)])
    for copy in copies:
        copy.wait()


ANY = pl.BlockSpec(memory_space=pl.ANY)
VMEM = pl.BlockSpec(memory_space=pltpu.VMEM)
SMEM = pl.BlockSpec(memory_space=pltpu.SMEM)


def assemble(arrays, where):
    return pl.pallas_call(
        assemble_kernel,
        out_shape=jax.ShapeDtypeStruct((NZ, 9 * SLAB, C), BF),
        in_specs=[SMEM, *[ANY] * len(arrays)],
        out_specs=VMEM,
        scratch_shapes=[pltpu.SemaphoreType.DMA((len(arrays),))],
        compiler_params=pltpu.CompilerParams(vmem_limit_bytes=12 * 2**20),
        name="assemble",
    )(where, *arrays)


def convolve(frames, rows, whole, wide):
    count = len(frames) - 2
    for t in range(3):
        left = jnp.concatenate(
            [
                jnp.concatenate(
                    [frames[t + f][k : k + rows].reshape(rows * 48, C) for f in range(count)], axis=0
                )
                for k in range(3)
            ],
            axis=1,
        )
        right = jnp.concatenate(
            [
                jnp.concatenate([whole(3 * t + k)[d * C : (d + 1) * C] for d in range(3)], axis=1)
                for k in range(3)
            ],
            axis=0,
        )
        part = jnp.dot(left, right, preferred_element_type=F32)
        if t == 0:
            wide[...] = part
        else:
            wide[...] += part
    column = lax.broadcasted_iota(jnp.int32, (48, C), 0)
    lines = []
    for i in range(count * rows):
        line = wide[48 * i : 48 * i + 48]
        before = jnp.where(column == 0, 0.0, pltpu.roll(line[:, :C], 1, 0))
        behind = jnp.where(column == 47, 0.0, pltpu.roll(line[:, 2 * C :], 47, 0))
        lines.append(before + line[:, C : 2 * C] + behind)
    return lines


def first_kernel(tile, earlier, grown, weight, bias, gain, out, wide):
    frames = [earlier[0], earlier[1], *(grown[f] for f in range(4))]
    lines = convolve(frames, 5, lambda tap: weight[tap], wide)
    for i, line in enumerate(lines):
        result = activate(line + bias[...], gain[...])
        if i % 5 == 0:
            result = jnp.where(tile[0] == 0, 0.0, result)
        if i % 5 == 4:
            result = jnp.where(tile[0] == NY * NX - 1, 0.0, result)
        out[i // 5, i % 5] = result.astype(BF)


def conv_first(earlier, grown, weight, bias, gain, tile):
    return pl.pallas_call(
        first_kernel,
        out_shape=jax.ShapeDtypeStruct((4, 5, 48, C), BF),
        in_specs=[SMEM] + [VMEM] * 5,
        out_specs=VMEM,
        scratch_shapes=[pltpu.VMEM((960, 3 * C), F32)],
        compiler_params=pltpu.CompilerParams(vmem_limit_bytes=20 * 2**20),
        cost_estimate=cost(960),
        name="conv_first",
    )(tile, earlier, grown, weight, bias, gain)


def slab_rows(weight, tap):
    return weight[:, SLAB * tap : SLAB * (tap + 1)].reshape(3 * C, C)


def second_kernel(start, low, high, weight, latent, bias, *refs):
    out, wide, done, sem = refs[-4:]
    frames = [low[0], low[1], high[0], high[1]]
    lines = convolve(frames, 3, lambda tap: slab_rows(weight, tap), wide)
    for i, line in enumerate(lines):
        at = start + 48 * i
        done[48 * i : 48 * i + 48] = (
            line + bias[...] + latent[at : at + 48].astype(F32)
        ).astype(BF)
    copy = pltpu.make_async_copy(done, out.at[pl.ds(start, 288)], sem)
    copy.start()
    copy.wait()


def conv_second(low, high, weight, latent, bias, partial):
    start = 288 if partial is None else 0
    return pl.pallas_call(
        functools.partial(second_kernel, start),
        out_shape=jax.ShapeDtypeStruct((576, C), BF),
        in_specs=[VMEM] * 5 + ([] if partial is None else [ANY]),
        out_specs=ANY,
        input_output_aliases={} if partial is None else {5: 0},
        scratch_shapes=[
            pltpu.VMEM((288, 3 * C), F32),
            pltpu.VMEM((288, C), BF),
            pltpu.SemaphoreType.DMA,
        ],
        compiler_params=pltpu.CompilerParams(vmem_limit_bytes=12 * 2**20),
        cost_estimate=cost(288),
        name="second_late" if start else "second_early",
    )(low, high, weight, latent, bias, *([] if partial is None else [partial]))


def cost(size):
    return pl.CostEstimate(
        flops=2 * size * 27 * C * C, bytes_accessed=27 * C * C * 2, transcendentals=0
    )


def local(latent, gain_first, weight_first, bias_first, gain_second, weight_second, bias_second):
    y, x, z, core = (lax.axis_index(name) for name in AXES)

    def starts(step):
        down, across = lax.rem(y + step + NY, NY), lax.rem(x + step + NX, NX)
        down, across = 2 * BLOCK * down, 2 * BLOCK * across + BLOCK
        return jnp.where(core == 0, down, across), jnp.where(core == 0, across, down)

    mine, other = zip(*(starts(step) for step in (0, -1, 1, 2)))
    where = jnp.stack([*mine, *other]).astype(jnp.int32)
    tile = (y * NX + x).astype(jnp.int32).reshape(1)
    row = lambda v: v.reshape(1, C)

    whole_first = lax.all_gather(weight_first, ("z", "c"), axis=2, tiled=True)
    first = activate(latent, gain_first).astype(BF)
    grown = grow_rows(first)
    pieces, last = gather(weight_second.reshape(9, 72, C), y, x, z, core, grown)
    earlier = send(after(grown[2:], pieces[0]), neighbours(0, 1))
    others = [send(v, SWAP) for v in pieces[:3]]

    scales = row(bias_first), row(gain_second), tile
    second = conv_first(earlier, grown, whole_first.reshape(9, 3 * C, C), *scales)
    second_low, second_high = second[:2], second[2:]
    second_earlier = send(second_high, neighbours(0, 1))
    far = after(pieces[3:], second)
    others += [send(v, SWAP) for v in far]
    whole_second = assemble([*pieces[:3], *far, *others, last], where)
    rest = whole_second, latent.reshape(576, C), row(bias_second)
    partial = conv_second(second_low, second_high, *rest, None)
    return conv_second(second_earlier, second_low, *rest, partial).reshape(4, 3, 48, C)


def solution(mesh):
    fine = Mesh(mesh.devices.reshape(NY, NX, NZ, 2), AXES)
    frames = P(("z", "c"), ("y", "x"), None, None)
    slices = P(None, None, ("z", "c"), None)
    return jax.shard_map(
        local,
        mesh=fine,
        in_specs=(frames, P(), slices, P(), P(), slices, P()),
        out_specs=frames,
        check_vma=False,
    )
```

```python
import functools

import jax
import jax.numpy as jnp
from jax import lax
from jax.experimental import pallas as pl
from jax.experimental.pallas import tpu as pltpu
from jax.sharding import Mesh
from jax.sharding import PartitionSpec as P

BF = jnp.bfloat16
F32 = jnp.float32
C = 384
NY, NX, NZ = 4, 4, 8
AXES = ("y", "x", "z", "c")
SLAB = 144
PART = 40
BLOCK = 160


def index(y, x, z, c):
    return ((y % NY * NX + x % NX) * NZ + z % NZ) * 2 + c


def perm(to):
    return [
        (index(y, x, z, c), index(*to(y, x, z, c)))
        for y in range(NY)
        for x in range(NX)
        for z in range(NZ)
        for c in range(2)
    ]


def along_z(steps):
    return perm(lambda y, x, z, c: (y, x, z + steps if c == 0 else z - steps, c))


SWAP = perm(lambda y, x, z, c: (y, x, z, 1 - c))
RING_UP = perm(lambda y, x, z, c: (y, x + 1, z, c) if c == 0 else (y + 1, x, z, c))
RING_DOWN = perm(lambda y, x, z, c: (y, x - 1, z, c) if c == 0 else (y - 1, x, z, c))

RING_FAR = perm(lambda y, x, z, c: (y, x + 2, z, c) if c == 0 else (y + 2, x, z, c))
CROSS_UP = perm(lambda y, x, z, c: (y + 1, x, z, c) if c == 0 else (y, x + 1, z, c))
CROSS_DOWN = perm(lambda y, x, z, c: (y - 1, x, z, c) if c == 0 else (y, x - 1, z, c))


def neighbours(tile_step, group_step):
    tiles, groups = NY * NX, NZ * 2
    return [
        (t * groups + g, (t + tile_step) * groups + g + group_step)
        for t in range(tiles)
        for g in range(groups)
        if 0 <= t + tile_step < tiles and 0 <= g + group_step < groups
    ]


def send(value, pairs):
    return lax.ppermute(value, AXES, pairs)


def activate(values, gain):
    wide = values.astype(F32)
    scaled = wide * lax.rsqrt(jnp.mean(wide * wide, axis=-1, keepdims=True) + 1e-06) * gain
    return jax.nn.silu(scaled)


def after(value, *others):
    return lax.optimization_barrier((value, others))[0]


def grow_rows(own):
    above = send(own[:, 1:], neighbours(1, 0))
    below = send(own[:, :2], neighbours(-1, 0))
    return [
        jnp.concatenate([above[k : k + 2], own[k : k + 2], below[k : k + 2]], axis=1) for k in (0, 2)
    ]


def gather(weight, y, x, z, core):
    first_core = core == 0
    other = send(weight, SWAP)
    slab = jnp.concatenate(
        [jnp.where(first_core, weight, other), jnp.where(first_core, other, weight)], axis=1
    ).reshape(9 * SLAB, C)
    starts = BLOCK * 2 * y + PART * x, BLOCK * 2 * x + BLOCK + PART * y
    both = jnp.concatenate(
        [*(lax.dynamic_slice_in_dim(slab, at, PART, axis=0) for at in starts), slab[8 * BLOCK :]],
        axis=0,
    )
    one, two, three, four = (send(both, along_z(steps)) for steps in (1, 2, 3, 4))
    sent = jnp.stack([one, two, three])
    other = send(sent, SWAP)
    plus, minus = jnp.where(first_core, other, sent), jnp.where(first_core, sent, other)
    parts = [both, plus[0], plus[1], plus[2], four, minus[2], minus[1], minus[0]]
    slabs = lax.dynamic_slice_in_dim(jnp.stack(parts + parts), lax.rem(NZ - z, NZ), NZ, axis=0)
    last = slabs[:, 2 * PART :]
    chunk = jnp.where(first_core, slabs[:, :PART], slabs[:, PART : 2 * PART])

    chunk, last = lax.optimization_barrier((chunk, last))
    parts = [chunk, *(send(chunk, pairs) for pairs in (RING_DOWN, RING_FAR, RING_UP))]
    spot = lax.rem(4 - jnp.where(first_core, x, y), 4)
    turned = lax.dynamic_slice_in_dim(jnp.stack(parts + parts), spot, 4, axis=0)
    chunk = turned.transpose(1, 0, 2, 3).reshape(NZ, BLOCK, C)
    low, high = chunk[: NZ // 2], chunk[NZ // 2 :]
    up_low, down_high = send(low, CROSS_UP), send(high, CROSS_DOWN)
    up_high, down_low = send(high, CROSS_UP), send(low, CROSS_DOWN)
    far = send(up_low, CROSS_UP), send(down_high, CROSS_DOWN)
    return [low, high, up_low, up_high, down_low, down_high, *far], last, both


def assemble_kernel(where, *refs):
    *arrays, last, whole, sems = refs
    copies = []

    def fetch(src, dst):
        copy = pltpu.make_async_copy(src, dst, sems.at[len(copies)])
        copy.start()
        copies.append(copy)

    half = NZ // 2
    for k, src in enumerate(arrays):
        at = pl.multiple_of(where[k // 2], BLOCK)
        fetch(src, whole.at[pl.ds(k % 2 * half, half), pl.ds(at, BLOCK)])
    fetch(last, whole.at[:, pl.ds(8 * BLOCK, 9 * SLAB - 8 * BLOCK)])
    for copy in copies:
        copy.wait()


ANY = pl.BlockSpec(memory_space=pl.ANY)
VMEM = pl.BlockSpec(memory_space=pltpu.VMEM)
SMEM = pl.BlockSpec(memory_space=pltpu.SMEM)


def assemble(arrays, where):
    return pl.pallas_call(
        assemble_kernel,
        out_shape=jax.ShapeDtypeStruct((NZ, 9 * SLAB, C), BF),
        in_specs=[SMEM, *[ANY] * len(arrays)],
        out_specs=VMEM,
        scratch_shapes=[pltpu.SemaphoreType.DMA((len(arrays),))],
        compiler_params=pltpu.CompilerParams(vmem_limit_bytes=12 * 2**20),
        name="assemble",
    )(where, *arrays)


def convolve(frames, rows, whole, wide):
    count = len(frames) - 2
    for t in range(3):
        left = jnp.concatenate(
            [
                jnp.concatenate(
                    [frames[t + f][k : k + rows].reshape(rows * 48, C) for f in range(count)], axis=0
                )
                for k in range(3)
            ],
            axis=1,
        )
        right = jnp.concatenate(
            [
                jnp.concatenate([whole(3 * t + k)[d * C : (d + 1) * C] for d in range(3)], axis=1)
                for k in range(3)
            ],
            axis=0,
        )
        part = jnp.dot(left, right, preferred_element_type=F32)
        if t == 0:
            wide[...] = part
        else:
            wide[...] += part
    column = lax.broadcasted_iota(jnp.int32, (48, C), 0)
    lines = []
    for i in range(count * rows):
        line = wide[48 * i : 48 * i + 48]
        before = jnp.where(column == 0, 0.0, pltpu.roll(line[:, :C], 1, 0))
        behind = jnp.where(column == 47, 0.0, pltpu.roll(line[:, 2 * C :], 47, 0))
        lines.append(before + line[:, C : 2 * C] + behind)
    return lines


def first_kernel(tile, earlier, low, high, weight, bias, gain, out, wide, kept, sems):
    copies = [
        pltpu.make_async_copy(weight.at[pl.ds(3 * t, 3)], kept.at[pl.ds(3 * t, 3)], sems.at[t])
        for t in range(3)
    ]
    for copy in copies:
        copy.start()

    arrived = set()

    def whole(tap):
        if tap // 3 not in arrived:
            arrived.add(tap // 3)
            copies[tap // 3].wait()
        return kept[tap]

    frames = [part[f] for part in (earlier, low, high) for f in range(2)]
    lines = convolve(frames, 5, whole, wide)
    for i, line in enumerate(lines):
        result = activate(line + bias[...], gain[...])
        if i % 5 == 0:
            result = jnp.where(tile[0] == 0, 0.0, result)
        if i % 5 == 4:
            result = jnp.where(tile[0] == NY * NX - 1, 0.0, result)
        out[i // 5, i % 5] = result.astype(BF)


def conv_first(earlier, low, high, weight, bias, gain, tile):
    return pl.pallas_call(
        first_kernel,
        out_shape=jax.ShapeDtypeStruct((4, 5, 48, C), BF),
        in_specs=[SMEM, VMEM, VMEM, VMEM, ANY, VMEM, VMEM],
        out_specs=VMEM,
        scratch_shapes=[
            pltpu.VMEM((960, 3 * C), F32),
            pltpu.VMEM((9, 3 * C, C), BF),
            pltpu.SemaphoreType.DMA((3,)),
        ],
        compiler_params=pltpu.CompilerParams(vmem_limit_bytes=54 * 2**20),
        cost_estimate=cost(960),
        name="conv_first",
    )(tile, earlier, low, high, weight, bias, gain)


def slab_rows(weight, tap):
    return weight[:, SLAB * tap : SLAB * (tap + 1)].reshape(3 * C, C)


def second_kernel(start, low, high, weight, latent, bias, *refs):
    out, wide, done, sem = refs[-4:]
    frames = [low[0], low[1], high[0], high[1]]
    lines = convolve(frames, 3, lambda tap: slab_rows(weight, tap), wide)
    for i, line in enumerate(lines):
        at = start + 48 * i
        done[48 * i : 48 * i + 48] = (
            line + bias[...] + latent[at : at + 48].astype(F32)
        ).astype(BF)
    copy = pltpu.make_async_copy(done, out.at[pl.ds(start, 288)], sem)
    copy.start()
    copy.wait()


def conv_second(low, high, weight, latent, bias, partial):
    start = 288 if partial is None else 0
    return pl.pallas_call(
        functools.partial(second_kernel, start),
        out_shape=jax.ShapeDtypeStruct((576, C), BF),
        in_specs=[VMEM] * 5 + ([] if partial is None else [ANY]),
        out_specs=ANY,
        input_output_aliases={} if partial is None else {5: 0},
        scratch_shapes=[
            pltpu.VMEM((288, 3 * C), F32),
            pltpu.VMEM((288, C), BF),
            pltpu.SemaphoreType.DMA,
        ],
        compiler_params=pltpu.CompilerParams(vmem_limit_bytes=12 * 2**20),
        cost_estimate=cost(288),
        name="second_late" if start else "second_early",
    )(low, high, weight, latent, bias, *([] if partial is None else [partial]))


def cost(size):
    return pl.CostEstimate(
        flops=2 * size * 27 * C * C, bytes_accessed=27 * C * C * 2, transcendentals=0
    )


def local(latent, gain_first, weight_first, bias_first, gain_second, weight_second, bias_second):
    y, x, z, core = (lax.axis_index(name) for name in AXES)

    def starts(step):
        down, across = lax.rem(y + step + NY, NY), lax.rem(x + step + NX, NX)
        down, across = 2 * BLOCK * down, 2 * BLOCK * across + BLOCK
        return jnp.where(core == 0, down, across), jnp.where(core == 0, across, down)

    mine, other = zip(*(starts(step) for step in (0, -1, 1, 2)))
    where = jnp.stack([*mine, *other]).astype(jnp.int32)
    tile = (y * NX + x).astype(jnp.int32).reshape(1)
    row = lambda v: v.reshape(1, C)

    whole_first = lax.all_gather(weight_first, ("z", "c"), axis=2, tiled=True)
    pieces, last, both = gather(weight_second.reshape(9, 72, C), y, x, z, core)
    first = activate(after(latent, both), gain_first).astype(BF)
    low, high = grow_rows(first)
    earlier = send(after(high, *pieces[:2]), neighbours(0, 1))
    others = [send(v, SWAP) for v in pieces[:6]]

    scales = row(bias_first), row(gain_second), tile
    second = conv_first(earlier, low, high, whole_first.reshape(9, 3 * C, C), *scales)
    second_low, second_high = second[:2], second[2:]
    second_earlier = send(second_high, neighbours(0, 1))
    far = after(pieces[6:], second)
    others += [send(v, SWAP) for v in far]
    whole_second = assemble([*pieces[:6], *far, *others, last], where)
    rest = whole_second, latent.reshape(576, C), row(bias_second)
    partial = conv_second(second_low, second_high, *rest, None)
    return conv_second(second_earlier, second_low, *rest, partial).reshape(4, 3, 48, C)


def solution(mesh):
    fine = Mesh(mesh.devices.reshape(NY, NX, NZ, 2), AXES)
    frames = P(("z", "c"), ("y", "x"), None, None)
    slices = P(None, None, ("z", "c"), None)
    return jax.shard_map(
        local,
        mesh=fine,
        in_specs=(frames, P(), slices, P(), P(), slices, P()),
        out_specs=frames,
        check_vma=False,
    )
```

```python
import functools

import jax
import jax.numpy as jnp
from jax import lax
from jax.experimental import pallas as pl
from jax.experimental.pallas import tpu as pltpu
from jax.sharding import Mesh
from jax.sharding import PartitionSpec as P

BF = jnp.bfloat16
F32 = jnp.float32
C = 384
NY, NX, NZ = 4, 4, 8
AXES = ("y", "x", "z", "c")
SLAB = 144
PART = 40
BLOCK = 160


def index(y, x, z, c):
    return ((y % NY * NX + x % NX) * NZ + z % NZ) * 2 + c


def perm(to):
    return [
        (index(y, x, z, c), index(*to(y, x, z, c)))
        for y in range(NY)
        for x in range(NX)
        for z in range(NZ)
        for c in range(2)
    ]


def along_z(steps):
    return perm(lambda y, x, z, c: (y, x, z + steps if c == 0 else z - steps, c))


SWAP = perm(lambda y, x, z, c: (y, x, z, 1 - c))
RING_UP = perm(lambda y, x, z, c: (y, x + 1, z, c) if c == 0 else (y + 1, x, z, c))
RING_DOWN = perm(lambda y, x, z, c: (y, x - 1, z, c) if c == 0 else (y - 1, x, z, c))

RING_FAR = perm(lambda y, x, z, c: (y, x + 2, z, c) if c == 0 else (y + 2, x, z, c))
CROSS_UP = perm(lambda y, x, z, c: (y + 1, x, z, c) if c == 0 else (y, x + 1, z, c))
CROSS_DOWN = perm(lambda y, x, z, c: (y - 1, x, z, c) if c == 0 else (y, x - 1, z, c))


def neighbours(tile_step, group_step):
    tiles, groups = NY * NX, NZ * 2
    return [
        (t * groups + g, (t + tile_step) * groups + g + group_step)
        for t in range(tiles)
        for g in range(groups)
        if 0 <= t + tile_step < tiles and 0 <= g + group_step < groups
    ]


def send(value, pairs):
    return lax.ppermute(value, AXES, pairs)


def activate(values, gain):
    wide = values.astype(F32)
    scaled = wide * lax.rsqrt(jnp.mean(wide * wide, axis=-1, keepdims=True) + 1e-06) * gain
    return jax.nn.silu(scaled)


def after(value, *others):
    return lax.optimization_barrier((value, others))[0]


def grow_rows(own):
    above = send(own[:, 1:], neighbours(1, 0))
    below = send(own[:, :2], neighbours(-1, 0))
    return [
        jnp.concatenate([above[k : k + 2], own[k : k + 2], below[k : k + 2]], axis=1) for k in (0, 2)
    ]


def gather(weight, y, x, z, core, rows):
    first_core = core == 0
    other = send(weight, SWAP)
    slab = jnp.concatenate(
        [jnp.where(first_core, weight, other), jnp.where(first_core, other, weight)], axis=1
    ).reshape(9 * SLAB, C)
    starts = BLOCK * 2 * y + PART * x, BLOCK * 2 * x + BLOCK + PART * y
    both = jnp.concatenate(
        [*(lax.dynamic_slice_in_dim(slab, at, PART, axis=0) for at in starts), slab[8 * BLOCK :]],
        axis=0,
    )
    one, two, three, four = (send(both, along_z(steps)) for steps in (1, 2, 3, 4))
    sent = jnp.stack([one, two, three])
    other = send(sent, SWAP)
    plus, minus = jnp.where(first_core, other, sent), jnp.where(first_core, sent, other)
    parts = [both, plus[0], plus[1], plus[2], four, minus[2], minus[1], minus[0]]
    slabs = lax.dynamic_slice_in_dim(jnp.stack(parts + parts), lax.rem(NZ - z, NZ), NZ, axis=0)
    last = slabs[:, 2 * PART :]
    chunk = jnp.where(first_core, slabs[:, :PART], slabs[:, PART : 2 * PART])

    chunk, last, _ = lax.optimization_barrier((chunk, last, rows(both)))
    parts = [chunk, *(send(chunk, pairs) for pairs in (RING_DOWN, RING_FAR, RING_UP))]
    spot = lax.rem(4 - jnp.where(first_core, x, y), 4)
    turned = lax.dynamic_slice_in_dim(jnp.stack(parts + parts), spot, 4, axis=0)
    chunk = turned.transpose(1, 0, 2, 3).reshape(NZ, BLOCK, C)
    low, high = chunk[: NZ // 2], chunk[NZ // 2 :]
    up_low, down_high = send(low, CROSS_UP), send(high, CROSS_DOWN)
    up_high, down_low = send(high, CROSS_UP), send(low, CROSS_DOWN)
    far = send(up_low, CROSS_UP), send(down_high, CROSS_DOWN)
    return [low, high, up_low, up_high, down_low, down_high, *far], last


def start_assembly(where, arrays, last, whole, sems):
    copies = []

    def fetch(src, dst):
        copy = pltpu.make_async_copy(src, dst, sems.at[len(copies)])
        copy.start()
        copies.append(copy)

    half = NZ // 2
    for k, src in enumerate(arrays):
        at = pl.multiple_of(where[k // 2], BLOCK)
        fetch(src, whole.at[pl.ds(k % 2 * half, half), pl.ds(at, BLOCK)])
    fetch(last, whole.at[:, pl.ds(8 * BLOCK, 9 * SLAB - 8 * BLOCK)])
    return copies


ANY = pl.BlockSpec(memory_space=pl.ANY)
VMEM = pl.BlockSpec(memory_space=pltpu.VMEM)
SMEM = pl.BlockSpec(memory_space=pltpu.SMEM)


def convolve(frames, rows, whole, wide):
    count = len(frames) - 2
    for t in range(3):
        left = jnp.concatenate(
            [
                jnp.concatenate(
                    [frames[t + f][k : k + rows].reshape(rows * 48, C) for f in range(count)], axis=0
                )
                for k in range(3)
            ],
            axis=1,
        )
        right = jnp.concatenate(
            [
                jnp.concatenate([whole(3 * t + k)[d * C : (d + 1) * C] for d in range(3)], axis=1)
                for k in range(3)
            ],
            axis=0,
        )
        part = jnp.dot(left, right, preferred_element_type=F32)
        if t == 0:
            wide[...] = part
        else:
            wide[...] += part
    column = lax.broadcasted_iota(jnp.int32, (48, C), 0)
    lines = []
    for i in range(count * rows):
        line = wide[48 * i : 48 * i + 48]
        before = jnp.where(column == 0, 0.0, pltpu.roll(line[:, :C], 1, 0))
        behind = jnp.where(column == 47, 0.0, pltpu.roll(line[:, 2 * C :], 47, 0))
        lines.append(before + line[:, C : 2 * C] + behind)
    return lines


def first_kernel(tile, where, earlier, low, high, weight, bias, gain, *refs):
    *arrays, last, out_low, out_high, next_weight, wide, sems = refs
    copies = start_assembly(where, arrays, last, next_weight, sems)
    frames = [part[f] for part in (earlier, low, high) for f in range(2)]
    lines = convolve(frames, 5, lambda tap: weight[tap], wide)
    for i, line in enumerate(lines):
        result = activate(line + bias[...], gain[...])
        if i % 5 == 0:
            result = jnp.where(tile[0] == 0, 0.0, result)
        if i % 5 == 4:
            result = jnp.where(tile[0] == NY * NX - 1, 0.0, result)
        out = out_low if i < 10 else out_high
        out[i // 5 % 2, i % 5] = result.astype(BF)
    for copy in copies:
        copy.wait()


def conv_first(tile, where, earlier, low, high, weight, bias, gain, pieces):
    half = jax.ShapeDtypeStruct((2, 5, 48, C), BF)
    return pl.pallas_call(
        first_kernel,
        out_shape=[half, half, jax.ShapeDtypeStruct((NZ, 9 * SLAB, C), BF)],
        in_specs=[SMEM, SMEM] + [VMEM] * 6 + [ANY] * len(pieces),
        out_specs=[VMEM] * 3,
        scratch_shapes=[pltpu.VMEM((960, 3 * C), F32), pltpu.SemaphoreType.DMA((len(pieces),))],
        compiler_params=pltpu.CompilerParams(vmem_limit_bytes=30 * 2**20),
        cost_estimate=cost(960),
        name="conv_first",
    )(tile, where, earlier, low, high, weight, bias, gain, *pieces)


def slab_rows(weight, tap):
    return weight[:, SLAB * tap : SLAB * (tap + 1)].reshape(3 * C, C)


def second_kernel(start, low, high, weight, latent, bias, *refs):
    out, wide, done, sem = refs[-4:]
    frames = [low[0], low[1], high[0], high[1]]
    lines = convolve(frames, 3, lambda tap: slab_rows(weight, tap), wide)
    for i, line in enumerate(lines):
        at = start + 48 * i
        done[48 * i : 48 * i + 48] = (
            line + bias[...] + latent[at : at + 48].astype(F32)
        ).astype(BF)
    copy = pltpu.make_async_copy(done, out.at[pl.ds(start, 288)], sem)
    copy.start()
    copy.wait()


def conv_second(low, high, weight, latent, bias, partial):
    start = 288 if partial is None else 0
    return pl.pallas_call(
        functools.partial(second_kernel, start),
        out_shape=jax.ShapeDtypeStruct((576, C), BF),
        in_specs=[VMEM] * 5 + ([] if partial is None else [ANY]),
        out_specs=ANY,
        input_output_aliases={} if partial is None else {5: 0},
        scratch_shapes=[
            pltpu.VMEM((288, 3 * C), F32),
            pltpu.VMEM((288, C), BF),
            pltpu.SemaphoreType.DMA,
        ],
        compiler_params=pltpu.CompilerParams(vmem_limit_bytes=12 * 2**20),
        cost_estimate=cost(288),
        name="second_late" if start else "second_early",
    )(low, high, weight, latent, bias, *([] if partial is None else [partial]))


def cost(size):
    return pl.CostEstimate(
        flops=2 * size * 27 * C * C, bytes_accessed=27 * C * C * 2, transcendentals=0
    )


def local(latent, gain_first, weight_first, bias_first, gain_second, weight_second, bias_second):
    y, x, z, core = (lax.axis_index(name) for name in AXES)

    def starts(step):
        down, across = lax.rem(y + step + NY, NY), lax.rem(x + step + NX, NX)
        down, across = 2 * BLOCK * down, 2 * BLOCK * across + BLOCK
        return jnp.where(core == 0, down, across), jnp.where(core == 0, across, down)

    mine, other = zip(*(starts(step) for step in (0, -1, 1, 2)))
    where = jnp.stack([*mine, *other]).astype(jnp.int32)
    tile = (y * NX + x).astype(jnp.int32).reshape(1)
    row = lambda v: v.reshape(1, C)

    whole_first = lax.all_gather(weight_first, ("z", "c"), axis=2, tiled=True)
    halo = []

    def rows(before):
        halo.extend(grow_rows(activate(after(latent, before), gain_first).astype(BF)))
        return halo

    pieces, last = gather(weight_second.reshape(9, 72, C), y, x, z, core, rows)
    low, high = halo
    earlier = send(high, neighbours(0, 1))
    pieces = [*pieces, *(send(v, SWAP) for v in pieces), last]

    second_low, second_high, whole_second = conv_first(
        tile,
        where,
        earlier,
        low,
        high,
        whole_first.reshape(9, 3 * C, C),
        row(bias_first),
        row(gain_second),
        pieces,
    )
    second_earlier = send(second_high, neighbours(0, 1))
    rest = whole_second, latent.reshape(576, C), row(bias_second)
    partial = conv_second(second_low, second_high, *rest, None)
    return conv_second(second_earlier, second_low, *rest, partial).reshape(4, 3, 48, C)


def solution(mesh):
    fine = Mesh(mesh.devices.reshape(NY, NX, NZ, 2), AXES)
    frames = P(("z", "c"), ("y", "x"), None, None)
    slices = P(None, None, ("z", "c"), None)
    return jax.shard_map(
        local,
        mesh=fine,
        in_specs=(frames, P(), slices, P(), P(), slices, P()),
        out_specs=frames,
        check_vma=False,
    )
```

```python
import functools

import jax
import jax.numpy as jnp
from jax import lax
from jax.experimental import pallas as pl
from jax.experimental.pallas import tpu as pltpu
from jax.sharding import Mesh
from jax.sharding import PartitionSpec as P

BF = jnp.bfloat16
F32 = jnp.float32
C = 384
NY, NX, NZ = 4, 4, 8
AXES = ("y", "x", "z", "c")
SLAB = 144
PART = 40
BLOCK = 160


def index(y, x, z, c):
    return ((y % NY * NX + x % NX) * NZ + z % NZ) * 2 + c


def perm(to):
    return [
        (index(y, x, z, c), index(*to(y, x, z, c)))
        for y in range(NY)
        for x in range(NX)
        for z in range(NZ)
        for c in range(2)
    ]


def along_z(steps):
    return perm(lambda y, x, z, c: (y, x, z + steps if c == 0 else z - steps, c))


SWAP = perm(lambda y, x, z, c: (y, x, z, 1 - c))
RING_UP = perm(lambda y, x, z, c: (y, x + 1, z, c) if c == 0 else (y + 1, x, z, c))
RING_DOWN = perm(lambda y, x, z, c: (y, x - 1, z, c) if c == 0 else (y - 1, x, z, c))

RING_FAR = perm(lambda y, x, z, c: (y, x + 2, z, c) if c == 0 else (y + 2, x, z, c))
CROSS_UP = perm(lambda y, x, z, c: (y + 1, x, z, c) if c == 0 else (y, x + 1, z, c))
CROSS_FAR = perm(lambda y, x, z, c: (y + 2, x, z, c) if c == 0 else (y, x + 2, z, c))
CROSS_DOWN = perm(lambda y, x, z, c: (y - 1, x, z, c) if c == 0 else (y, x - 1, z, c))


def neighbours(tile_step, group_step):
    tiles, groups = NY * NX, NZ * 2
    return [
        (t * groups + g, (t + tile_step) * groups + g + group_step)
        for t in range(tiles)
        for g in range(groups)
        if 0 <= t + tile_step < tiles and 0 <= g + group_step < groups
    ]


def send(value, pairs):
    return lax.ppermute(value, AXES, pairs)


def activate(values, gain):
    wide = values.astype(F32)
    scaled = wide * lax.rsqrt(jnp.mean(wide * wide, axis=-1, keepdims=True) + 1e-06) * gain
    return jax.nn.silu(scaled)


def after(value, *others):
    return lax.optimization_barrier((value, others))[0]


def grow_rows(own):
    above = send(own[:, 1:], neighbours(1, 0))
    below = send(own[:, :2], neighbours(-1, 0))
    return [
        jnp.concatenate([above[k : k + 2], own[k : k + 2], below[k : k + 2]], axis=1) for k in (0, 2)
    ]


def gather(weight, y, x, z, core, rows):
    first_core = core == 0
    other = send(weight, SWAP)
    slab = jnp.concatenate(
        [jnp.where(first_core, weight, other), jnp.where(first_core, other, weight)], axis=1
    ).reshape(9 * SLAB, C)
    starts = BLOCK * 2 * y + PART * x, BLOCK * 2 * x + BLOCK + PART * y
    both = jnp.concatenate(
        [*(lax.dynamic_slice_in_dim(slab, at, PART, axis=0) for at in starts), slab[8 * BLOCK :]],
        axis=0,
    )
    one, two, three, four = (send(both, along_z(steps)) for steps in (1, 2, 3, 4))
    sent = jnp.stack([one, two, three])
    other = send(sent, SWAP)
    plus, minus = jnp.where(first_core, other, sent), jnp.where(first_core, sent, other)
    parts = [both, plus[0], plus[1], plus[2], four, minus[2], minus[1], minus[0]]
    slabs = lax.dynamic_slice_in_dim(jnp.stack(parts + parts), lax.rem(NZ - z, NZ), NZ, axis=0)
    last = slabs[:, 2 * PART :]
    chunk = jnp.where(first_core, slabs[:, :PART], slabs[:, PART : 2 * PART])

    halo = rows(both)
    chunk, last, _ = lax.optimization_barrier((chunk, last, halo))
    parts = [chunk, *(send(chunk, pairs) for pairs in (RING_DOWN, RING_FAR, RING_UP))]
    spot = lax.rem(4 - jnp.where(first_core, x, y), 4)
    turned = lax.dynamic_slice_in_dim(jnp.stack(parts + parts), spot, 4, axis=0)
    chunk = turned.transpose(1, 0, 2, 3).reshape(NZ, BLOCK, C)
    up, down = send(chunk, CROSS_UP), send(chunk, CROSS_DOWN)
    far = send(after(chunk, up, down), CROSS_FAR)
    return [chunk, up, down, far], last, halo


ANY = pl.BlockSpec(memory_space=pl.ANY)
VMEM = pl.BlockSpec(memory_space=pltpu.VMEM)
SMEM = pl.BlockSpec(memory_space=pltpu.SMEM)


def convolve(frames, rows, whole, wide):
    count = len(frames) - 2
    for t in range(3):
        left = jnp.concatenate(
            [
                jnp.concatenate(
                    [frames[t + f][k : k + rows].reshape(rows * 48, C) for f in range(count)], axis=0
                )
                for k in range(3)
            ],
            axis=1,
        )
        right = jnp.concatenate(
            [
                jnp.concatenate([whole(3 * t + k)[d * C : (d + 1) * C] for d in range(3)], axis=1)
                for k in range(3)
            ],
            axis=0,
        )
        part = jnp.dot(left, right, preferred_element_type=F32)
        if t == 0:
            wide[...] = part
        else:
            wide[...] += part
    column = lax.broadcasted_iota(jnp.int32, (48, C), 0)
    lines = []
    for i in range(count * rows):
        line = wide[48 * i : 48 * i + 48]
        before = jnp.where(column == 0, 0.0, pltpu.roll(line[:, :C], 1, 0))
        behind = jnp.where(column == 47, 0.0, pltpu.roll(line[:, 2 * C :], 47, 0))
        lines.append(before + line[:, C : 2 * C] + behind)
    return lines


def first_kernel(tile, earlier, low, high, weight, bias, gain, out_low, out_high, wide):
    frames = [part[f] for part in (earlier, low, high) for f in range(2)]
    lines = convolve(frames, 5, lambda tap: weight[tap], wide)
    for i, line in enumerate(lines):
        result = activate(line + bias[...], gain[...])
        if i % 5 == 0:
            result = jnp.where(tile[0] == 0, 0.0, result)
        if i % 5 == 4:
            result = jnp.where(tile[0] == NY * NX - 1, 0.0, result)
        out = out_low if i < 10 else out_high
        out[i // 5 % 2, i % 5] = result.astype(BF)


def conv_first(tile, earlier, low, high, weight, bias, gain):
    half = jax.ShapeDtypeStruct((2, 5, 48, C), BF)
    return pl.pallas_call(
        first_kernel,
        out_shape=[half, half],
        in_specs=[SMEM] + [VMEM] * 6,
        out_specs=[VMEM, VMEM],
        scratch_shapes=[pltpu.VMEM((960, 3 * C), F32)],
        compiler_params=pltpu.CompilerParams(vmem_limit_bytes=20 * 2**20),
        cost_estimate=cost(960),
        name="conv_first",
    )(tile, earlier, low, high, weight, bias, gain)


def slab_rows(weight, tap):
    return weight[:, SLAB * tap : SLAB * (tap + 1)].reshape(3 * C, C)


def assembled(where, arrays, last, whole, sems):
    def start(block, index):
        @pl.when(where[index] == block * BLOCK)
        def _():
            rows = whole.at[:, pl.ds(block * BLOCK, BLOCK)]
            pltpu.make_async_copy(arrays[index], rows, sems.at[block]).start()

    for block in range(8):
        for index in range(8):
            start(block, index)
    rest = whole.at[:, pl.ds(8 * BLOCK, 9 * SLAB - 8 * BLOCK)]
    pltpu.make_async_copy(last, rest, sems.at[8]).start()
    arrived = set()

    def rows(tap):
        for block in range(SLAB * tap // BLOCK, -(-SLAB * (tap + 1) // BLOCK)):
            if block not in arrived:
                arrived.add(block)
                at = whole.at[:, pl.ds(block * BLOCK, BLOCK)] if block < 8 else rest
                pltpu.make_async_copy(at, at, sems.at[block]).wait()
        return slab_rows(whole, tap)

    return rows


def finish(lines, start, latent, bias, out, done, sem):
    for i, line in enumerate(lines):
        at = start + 48 * i
        done[48 * i : 48 * i + 48] = (
            line + bias[...] + latent[at : at + 48].astype(F32)
        ).astype(BF)
    copy = pltpu.make_async_copy(done, out.at[pl.ds(start, 288)], sem)
    copy.start()
    copy.wait()


def late_kernel(where, low, high, latent, bias, *refs):
    *arrays, last, out, whole, wide, done, sems, sem = refs
    rows = assembled(where, arrays, last, whole, sems)
    frames = [part[f] for part in (low, high) for f in range(2)]
    finish(convolve(frames, 3, rows, wide), 288, latent, bias, out, done, sem)


def early_kernel(low, high, latent, bias, weight, partial, out, wide, done, sem):
    frames = [part[f] for part in (low, high) for f in range(2)]
    lines = convolve(frames, 3, lambda tap: slab_rows(weight, tap), wide)
    finish(lines, 0, latent, bias, out, done, sem)


SCRATCH = [pltpu.VMEM((288, 3 * C), F32), pltpu.VMEM((288, C), BF)]


def conv_late(where, low, high, latent, bias, pieces):
    return pl.pallas_call(
        late_kernel,
        out_shape=[
            jax.ShapeDtypeStruct((576, C), BF),
            jax.ShapeDtypeStruct((NZ, 9 * SLAB, C), BF),
        ],
        in_specs=[SMEM] + [VMEM] * 4 + [ANY] * len(pieces),
        out_specs=[ANY, VMEM],
        scratch_shapes=[*SCRATCH, pltpu.SemaphoreType.DMA((9,)), pltpu.SemaphoreType.DMA],
        compiler_params=pltpu.CompilerParams(vmem_limit_bytes=20 * 2**20),
        cost_estimate=cost(288),
        name="second_late",
    )(where, low, high, latent, bias, *pieces)


def conv_early(low, high, latent, bias, weight, partial):
    return pl.pallas_call(
        early_kernel,
        out_shape=jax.ShapeDtypeStruct((576, C), BF),
        in_specs=[VMEM] * 5 + [ANY],
        out_specs=ANY,
        input_output_aliases={5: 0},
        scratch_shapes=[*SCRATCH, pltpu.SemaphoreType.DMA],
        compiler_params=pltpu.CompilerParams(vmem_limit_bytes=12 * 2**20),
        cost_estimate=cost(288),
        name="second_early",
    )(low, high, latent, bias, weight, partial)


def cost(size):
    return pl.CostEstimate(
        flops=2 * size * 27 * C * C, bytes_accessed=27 * C * C * 2, transcendentals=0
    )


def local(latent, gain_first, weight_first, bias_first, gain_second, weight_second, bias_second):
    y, x, z, core = (lax.axis_index(name) for name in AXES)

    def starts(step):
        down, across = lax.rem(y + step + NY, NY), lax.rem(x + step + NX, NX)
        down, across = 2 * BLOCK * down, 2 * BLOCK * across + BLOCK
        return jnp.where(core == 0, down, across), jnp.where(core == 0, across, down)

    mine, other = zip(*(starts(step) for step in (0, -1, 1, 2)))
    where = jnp.stack([*mine, *other]).astype(jnp.int32)
    tile = (y * NX + x).astype(jnp.int32).reshape(1)
    row = lambda v: v.reshape(1, C)

    whole_first = lax.all_gather(weight_first, ("z", "c"), axis=2, tiled=True)

    def rows(before):
        return grow_rows(activate(after(latent, before), gain_first).astype(BF))

    pieces, last, (low, high) = gather(weight_second.reshape(9, 72, C), y, x, z, core, rows)
    earlier = send(after(high, pieces[0]), neighbours(0, 1))
    others = [send(v, SWAP) for v in pieces[:3]]

    second_low, second_high = conv_first(
        tile, earlier, low, high, whole_first.reshape(9, 3 * C, C), row(bias_first), row(gain_second)
    )
    second_earlier = send(second_high, neighbours(0, 1))
    pieces[3] = after(pieces[3], second_high)
    others.append(send(pieces[3], SWAP))
    rest = latent.reshape(576, C), row(bias_second)
    partial, whole_second = conv_late(
        where, second_low, second_high, *rest, [*pieces, *others, last]
    )
    result = conv_early(second_earlier, second_low, *rest, whole_second, partial)
    return result.reshape(4, 3, 48, C)


def solution(mesh):
    fine = Mesh(mesh.devices.reshape(NY, NX, NZ, 2), AXES)
    frames = P(("z", "c"), ("y", "x"), None, None)
    slices = P(None, None, ("z", "c"), None)
    return jax.shard_map(
        local,
        mesh=fine,
        in_specs=(frames, P(), slices, P(), P(), slices, P()),
        out_specs=frames,
        check_vma=False,
    )
```

```python
import functools

import jax
import jax.numpy as jnp
from jax import lax
from jax.experimental import pallas as pl
from jax.experimental.pallas import tpu as pltpu
from jax.sharding import Mesh
from jax.sharding import PartitionSpec as P

BF = jnp.bfloat16
F32 = jnp.float32
C = 384
NY, NX, NZ = 4, 4, 8
AXES = ("y", "x", "z", "c")
SLAB = 144
PART = 40
BLOCK = 160


def index(y, x, z, c):
    return ((y % NY * NX + x % NX) * NZ + z % NZ) * 2 + c


def perm(to):
    return [
        (index(y, x, z, c), index(*to(y, x, z, c)))
        for y in range(NY)
        for x in range(NX)
        for z in range(NZ)
        for c in range(2)
    ]


def along_z(steps):
    return perm(lambda y, x, z, c: (y, x, z + steps if c == 0 else z - steps, c))


SWAP = perm(lambda y, x, z, c: (y, x, z, 1 - c))
RING_UP = perm(lambda y, x, z, c: (y, x + 1, z, c) if c == 0 else (y + 1, x, z, c))
RING_DOWN = perm(lambda y, x, z, c: (y, x - 1, z, c) if c == 0 else (y - 1, x, z, c))

RING_FAR = perm(lambda y, x, z, c: (y, x + 2, z, c) if c == 0 else (y + 2, x, z, c))
CROSS_UP = perm(lambda y, x, z, c: (y + 1, x, z, c) if c == 0 else (y, x + 1, z, c))
CROSS_FAR = perm(lambda y, x, z, c: (y + 2, x, z, c) if c == 0 else (y, x + 2, z, c))
CROSS_DOWN = perm(lambda y, x, z, c: (y - 1, x, z, c) if c == 0 else (y, x - 1, z, c))


def neighbours(tile_step, group_step):
    tiles, groups = NY * NX, NZ * 2
    return [
        (t * groups + g, (t + tile_step) * groups + g + group_step)
        for t in range(tiles)
        for g in range(groups)
        if 0 <= t + tile_step < tiles and 0 <= g + group_step < groups
    ]


def send(value, pairs):
    return lax.ppermute(value, AXES, pairs)


def activate(values, gain):
    wide = values.astype(F32)
    scaled = wide * lax.rsqrt(jnp.mean(wide * wide, axis=-1, keepdims=True) + 1e-06) * gain
    return jax.nn.silu(scaled)


def after(value, *others):
    return lax.optimization_barrier((value, others))[0]


def grow(own, before):
    own = after(jnp.concatenate([send(own[2:], neighbours(0, 1)), own], axis=0), before)
    above = send(own[:, 1:], neighbours(1, 0))
    below = send(own[:, :2], neighbours(-1, 0))
    return jnp.concatenate([above, own, below], axis=1)


def gather(weight, y, x, z, core, first):
    first_core = core == 0
    other = send(weight, SWAP)
    slab = jnp.concatenate(
        [jnp.where(first_core, weight, other), jnp.where(first_core, other, weight)], axis=1
    ).reshape(9 * SLAB, C)
    starts = BLOCK * 2 * y + PART * x, BLOCK * 2 * x + BLOCK + PART * y
    both = jnp.concatenate(
        [*(lax.dynamic_slice_in_dim(slab, at, PART, axis=0) for at in starts), slab[8 * BLOCK :]],
        axis=0,
    )
    one, two, three, four = (send(both, along_z(steps)) for steps in (1, 2, 3, 4))
    sent = jnp.stack([one, two, three])
    other = send(sent, SWAP)
    plus, minus = jnp.where(first_core, other, sent), jnp.where(first_core, sent, other)
    parts = [both, plus[0], plus[1], plus[2], four, minus[2], minus[1], minus[0]]
    slabs = lax.dynamic_slice_in_dim(jnp.stack(parts + parts), lax.rem(NZ - z, NZ), NZ, axis=0)
    last = slabs[:, 2 * PART :]
    chunk = jnp.where(first_core, slabs[:, :PART], slabs[:, PART : 2 * PART])

    grown = grow(first, both)
    chunk, last = lax.optimization_barrier((chunk, last))
    parts = [chunk, *(send(chunk, pairs) for pairs in (RING_DOWN, RING_FAR, RING_UP))]
    spot = lax.rem(4 - jnp.where(first_core, x, y), 4)
    turned = lax.dynamic_slice_in_dim(jnp.stack(parts + parts), spot, 4, axis=0)
    chunk = turned.transpose(1, 0, 2, 3).reshape(NZ, BLOCK, C)
    chunk = after(chunk, grown)
    up, down = send(chunk, CROSS_UP), send(chunk, CROSS_DOWN)
    far = send(after(chunk, up, down), CROSS_FAR)
    others = [send(v, SWAP) for v in (chunk, up, down)]
    return [chunk, up, down, *others, last], far, grown


ANY = pl.BlockSpec(memory_space=pl.ANY)
VMEM = pl.BlockSpec(memory_space=pltpu.VMEM)
SMEM = pl.BlockSpec(memory_space=pltpu.SMEM)


def convolve(frames, rows, whole, wide):
    count = len(frames) - 2
    for t in range(3):
        left = jnp.concatenate(
            [
                jnp.concatenate(
                    [frames[t + f][k : k + rows].reshape(rows * 48, C) for f in range(count)], axis=0
                )
                for k in range(3)
            ],
            axis=1,
        )
        right = jnp.concatenate(
            [
                jnp.concatenate([whole(3 * t + k)[d * C : (d + 1) * C] for d in range(3)], axis=1)
                for k in range(3)
            ],
            axis=0,
        )
        part = jnp.dot(left, right, preferred_element_type=F32)
        if t == 0:
            wide[...] = part
        else:
            wide[...] += part
    column = lax.broadcasted_iota(jnp.int32, (48, C), 0)
    lines = []
    for i in range(count * rows):
        line = wide[48 * i : 48 * i + 48]
        before = jnp.where(column == 0, 0.0, pltpu.roll(line[:, :C], 1, 0))
        behind = jnp.where(column == 47, 0.0, pltpu.roll(line[:, 2 * C :], 47, 0))
        lines.append(before + line[:, C : 2 * C] + behind)
    return lines


def first_kernel(tile, where, grown, weight, bias, gain, *refs):
    *arrays, last, out_low, out_high, next_weight, wide, sems = refs
    copies = []
    for k, src in enumerate([*arrays, last]):
        if src is last:
            rows = pl.ds(8 * BLOCK, 9 * SLAB - 8 * BLOCK)
        else:
            rows = pl.ds(pl.multiple_of(where[k + k // 3], BLOCK), BLOCK)
        copies.append(pltpu.make_async_copy(src, next_weight.at[:, rows], sems.at[k]))
        copies[k].start()
    lines = convolve([grown[f] for f in range(6)], 5, lambda tap: weight[tap], wide)
    for i, line in enumerate(lines):
        result = activate(line + bias[...], gain[...])
        if i % 5 == 0:
            result = jnp.where(tile[0] == 0, 0.0, result)
        if i % 5 == 4:
            result = jnp.where(tile[0] == NY * NX - 1, 0.0, result)
        out = out_low if i < 10 else out_high
        out[i // 5 % 2, i % 5] = result.astype(BF)
    for copy in copies:
        copy.wait()


def conv_first(tile, where, grown, weight, bias, gain, pieces):
    half = jax.ShapeDtypeStruct((2, 5, 48, C), BF)
    return pl.pallas_call(
        first_kernel,
        out_shape=[half, half, jax.ShapeDtypeStruct((NZ, 9 * SLAB, C), BF)],
        in_specs=[SMEM, SMEM] + [VMEM] * 4 + [ANY] * len(pieces),
        out_specs=[VMEM] * 3,
        scratch_shapes=[pltpu.VMEM((960, 3 * C), F32), pltpu.SemaphoreType.DMA((len(pieces),))],
        compiler_params=pltpu.CompilerParams(vmem_limit_bytes=30 * 2**20),
        cost_estimate=cost(960),
        name="conv_first",
    )(tile, where, grown, weight, bias, gain, *pieces)


def slab_rows(weight, tap):
    return weight[:, SLAB * tap : SLAB * (tap + 1)].reshape(3 * C, C)


def finish(lines, start, latent, bias, out, done, sem):
    for i, line in enumerate(lines):
        at = start + 48 * i
        done[48 * i : 48 * i + 48] = (
            line + bias[...] + latent[at : at + 48].astype(F32)
        ).astype(BF)
    copy = pltpu.make_async_copy(done, out.at[pl.ds(start, 288)], sem)
    copy.start()
    copy.wait()


def late_kernel(where, low, high, latent, bias, weight, far, other_far, out, whole, wide, done, sem):
    whole[...] = weight[...]
    for k, src in enumerate((far, other_far)):
        rows = pl.ds(pl.multiple_of(where[3 + 4 * k], BLOCK), BLOCK)
        whole[:, rows] = src[...]
    frames = [part[f] for part in (low, high) for f in range(2)]
    lines = convolve(frames, 3, lambda tap: slab_rows(whole, tap), wide)
    finish(lines, 288, latent, bias, out, done, sem)


def early_kernel(low, high, latent, bias, weight, partial, out, wide, done, sem):
    frames = [part[f] for part in (low, high) for f in range(2)]
    lines = convolve(frames, 3, lambda tap: slab_rows(weight, tap), wide)
    finish(lines, 0, latent, bias, out, done, sem)


SCRATCH = [pltpu.VMEM((288, 3 * C), F32), pltpu.VMEM((288, C), BF)]


def conv_late(where, low, high, latent, bias, weight, far, other_far):
    return pl.pallas_call(
        late_kernel,
        out_shape=[jax.ShapeDtypeStruct((576, C), BF), jax.ShapeDtypeStruct(weight.shape, BF)],
        in_specs=[SMEM] + [VMEM] * 7,
        out_specs=[ANY, VMEM],
        scratch_shapes=[*SCRATCH, pltpu.SemaphoreType.DMA],
        compiler_params=pltpu.CompilerParams(vmem_limit_bytes=20 * 2**20),
        cost_estimate=cost(288),
        name="second_late",
    )(where, low, high, latent, bias, weight, far, other_far)


def conv_early(low, high, latent, bias, weight, partial):
    return pl.pallas_call(
        early_kernel,
        out_shape=jax.ShapeDtypeStruct((576, C), BF),
        in_specs=[VMEM] * 5 + [ANY],
        out_specs=ANY,
        input_output_aliases={5: 0},
        scratch_shapes=[*SCRATCH, pltpu.SemaphoreType.DMA],
        compiler_params=pltpu.CompilerParams(vmem_limit_bytes=12 * 2**20),
        cost_estimate=cost(288),
        name="second_early",
    )(low, high, latent, bias, weight, partial)


def cost(size):
    return pl.CostEstimate(
        flops=2 * size * 27 * C * C, bytes_accessed=27 * C * C * 2, transcendentals=0
    )


def local(latent, gain_first, weight_first, bias_first, gain_second, weight_second, bias_second):
    y, x, z, core = (lax.axis_index(name) for name in AXES)

    def starts(step):
        down, across = lax.rem(y + step + NY, NY), lax.rem(x + step + NX, NX)
        down, across = 2 * BLOCK * down, 2 * BLOCK * across + BLOCK
        return jnp.where(core == 0, down, across), jnp.where(core == 0, across, down)

    mine, other = zip(*(starts(step) for step in (0, -1, 1, 2)))
    where = jnp.stack([*mine, *other]).astype(jnp.int32)
    tile = (y * NX + x).astype(jnp.int32).reshape(1)
    row = lambda v: v.reshape(1, C)

    whole_first = lax.all_gather(weight_first, ("z", "c"), axis=2, tiled=True)
    first = activate(latent, gain_first).astype(BF)
    pieces, far, grown = gather(weight_second.reshape(9, 72, C), y, x, z, core, first)

    second_low, second_high, most = conv_first(
        tile,
        where,
        grown,
        whole_first.reshape(9, 3 * C, C),
        row(bias_first),
        row(gain_second),
        pieces,
    )
    second_earlier = send(second_high, neighbours(0, 1))
    far = after(far, second_high)
    rest = latent.reshape(576, C), row(bias_second)
    partial, whole_second = conv_late(
        where, second_low, second_high, *rest, most, far, send(far, SWAP)
    )
    result = conv_early(second_earlier, second_low, *rest, whole_second, partial)
    return result.reshape(4, 3, 48, C)


def solution(mesh):
    fine = Mesh(mesh.devices.reshape(NY, NX, NZ, 2), AXES)
    frames = P(("z", "c"), ("y", "x"), None, None)
    slices = P(None, None, ("z", "c"), None)
    return jax.shard_map(
        local,
        mesh=fine,
        in_specs=(frames, P(), slices, P(), P(), slices, P()),
        out_specs=frames,
        check_vma=False,
    )
```

```python
import functools

import jax
import jax.numpy as jnp
from jax import lax
from jax.experimental import pallas as pl
from jax.experimental.pallas import tpu as pltpu
from jax.sharding import Mesh
from jax.sharding import PartitionSpec as P

BF = jnp.bfloat16
F32 = jnp.float32
C = 384
NY, NX, NZ = 4, 4, 8
AXES = ("y", "x", "z", "c")
SLAB = 144
PART = 40
BLOCK = 160


def index(y, x, z, c):
    return ((y % NY * NX + x % NX) * NZ + z % NZ) * 2 + c


def perm(to):
    return [
        (index(y, x, z, c), index(*to(y, x, z, c)))
        for y in range(NY)
        for x in range(NX)
        for z in range(NZ)
        for c in range(2)
    ]


def along_z(steps):
    return perm(lambda y, x, z, c: (y, x, z + steps if c == 0 else z - steps, c))


SWAP = perm(lambda y, x, z, c: (y, x, z, 1 - c))
RING_UP = perm(lambda y, x, z, c: (y, x + 1, z, c) if c == 0 else (y + 1, x, z, c))
RING_DOWN = perm(lambda y, x, z, c: (y, x - 1, z, c) if c == 0 else (y - 1, x, z, c))

RING_FAR = perm(lambda y, x, z, c: (y, x + 2, z, c) if c == 0 else (y + 2, x, z, c))
CROSS_UP = perm(lambda y, x, z, c: (y + 1, x, z, c) if c == 0 else (y, x + 1, z, c))
CROSS_FAR = perm(lambda y, x, z, c: (y + 2, x, z, c) if c == 0 else (y, x + 2, z, c))
CROSS_DOWN = perm(lambda y, x, z, c: (y - 1, x, z, c) if c == 0 else (y, x - 1, z, c))


def neighbours(tile_step, group_step):
    tiles, groups = NY * NX, NZ * 2
    return [
        (t * groups + g, (t + tile_step) * groups + g + group_step)
        for t in range(tiles)
        for g in range(groups)
        if 0 <= t + tile_step < tiles and 0 <= g + group_step < groups
    ]


def send(value, pairs):
    return lax.ppermute(value, AXES, pairs)


def activate(values, gain):
    wide = values.astype(F32)
    scaled = wide * lax.rsqrt(jnp.mean(wide * wide, axis=-1, keepdims=True) + 1e-06) * gain
    return jax.nn.silu(scaled)


def after(value, *others):
    return lax.optimization_barrier((value, others))[0]


def grow(own, before):
    own = after(jnp.concatenate([send(own[2:], neighbours(0, 1)), own], axis=0), before)
    above = send(own[:, 1:], neighbours(1, 0))
    below = send(own[:, :2], neighbours(-1, 0))
    return jnp.concatenate([above, own, below], axis=1)


def gather(weight, y, x, z, core, first):
    first_core = core == 0
    other = send(weight, SWAP)
    slab = jnp.concatenate(
        [jnp.where(first_core, weight, other), jnp.where(first_core, other, weight)], axis=1
    ).reshape(9 * SLAB, C)
    starts = BLOCK * 2 * y + PART * x, BLOCK * 2 * x + BLOCK + PART * y
    both = jnp.concatenate(
        [*(lax.dynamic_slice_in_dim(slab, at, PART, axis=0) for at in starts), slab[8 * BLOCK :]],
        axis=0,
    )
    one, two, three, four = (send(both, along_z(steps)) for steps in (1, 2, 3, 4))
    sent = jnp.stack([one, two, three])
    other = send(sent, SWAP)
    plus, minus = jnp.where(first_core, other, sent), jnp.where(first_core, sent, other)
    parts = [both, plus[0], plus[1], plus[2], four, minus[2], minus[1], minus[0]]
    slabs = lax.dynamic_slice_in_dim(jnp.stack(parts + parts), lax.rem(NZ - z, NZ), NZ, axis=0)
    last = slabs[:, 2 * PART :]
    chunk = jnp.where(first_core, slabs[:, :PART], slabs[:, PART : 2 * PART])

    grown = grow(first, both)
    chunk, last = lax.optimization_barrier((chunk, last))
    parts = [chunk, *(send(chunk, pairs) for pairs in (RING_DOWN, RING_FAR, RING_UP))]
    spot = lax.rem(4 - jnp.where(first_core, x, y), 4)
    turned = lax.dynamic_slice_in_dim(jnp.stack(parts + parts), spot, 4, axis=0)
    chunk = turned.transpose(1, 0, 2, 3).reshape(NZ, BLOCK, C)
    chunk = after(chunk, grown)
    up, down = send(chunk, CROSS_UP), send(chunk, CROSS_DOWN)
    far = send(after(chunk, up, down), CROSS_FAR)
    others = [send(v, SWAP) for v in (chunk, up, down)]
    return [chunk, up, down, *others, last], far, grown


ANY = pl.BlockSpec(memory_space=pl.ANY)
VMEM = pl.BlockSpec(memory_space=pltpu.VMEM)
SMEM = pl.BlockSpec(memory_space=pltpu.SMEM)


def convolve(frames, rows, whole, wide):
    count = len(frames) - 2

    def left(t, k):
        shown = [frames[t + f][k : k + rows].reshape(rows * 48, C) for f in range(count)]
        return jnp.concatenate(shown, axis=0)

    def right(t, k):
        tap = whole(3 * t + k)
        return jnp.concatenate([tap[d * C : (d + 1) * C] for d in range(3)], axis=1)

    taps = [(t, k) for t in range(3) for k in range(3)]
    wide[...] = jnp.dot(
        jnp.concatenate([left(t, k) for t, k in taps], axis=1),
        jnp.concatenate([right(t, k) for t, k in taps], axis=0),
        preferred_element_type=F32,
    )
    column = lax.broadcasted_iota(jnp.int32, (48, C), 0)
    lines = []
    for i in range(count * rows):
        line = wide[48 * i : 48 * i + 48]
        before = jnp.where(column == 0, 0.0, pltpu.roll(line[:, :C], 1, 0))
        behind = jnp.where(column == 47, 0.0, pltpu.roll(line[:, 2 * C :], 47, 0))
        lines.append(before + line[:, C : 2 * C] + behind)
    return lines


def first_kernel(tile, where, grown, weight, bias, gain, *refs):
    *arrays, last, out_low, out_high, next_weight, wide, sems = refs
    copies = []
    for k, src in enumerate([*arrays, last]):
        if src is last:
            rows = pl.ds(8 * BLOCK, 9 * SLAB - 8 * BLOCK)
        else:
            rows = pl.ds(pl.multiple_of(where[k + k // 3], BLOCK), BLOCK)
        copies.append(pltpu.make_async_copy(src, next_weight.at[:, rows], sems.at[k]))
        copies[k].start()
    lines = convolve([grown[f] for f in range(6)], 5, lambda tap: weight[tap], wide)
    for i, line in enumerate(lines):
        result = activate(line + bias[...], gain[...])
        if i % 5 == 0:
            result = jnp.where(tile[0] == 0, 0.0, result)
        if i % 5 == 4:
            result = jnp.where(tile[0] == NY * NX - 1, 0.0, result)
        out = out_low if i < 10 else out_high
        out[i // 5 % 2, i % 5] = result.astype(BF)
    for copy in copies:
        copy.wait()


def conv_first(tile, where, grown, weight, bias, gain, pieces):
    half = jax.ShapeDtypeStruct((2, 5, 48, C), BF)
    return pl.pallas_call(
        first_kernel,
        out_shape=[half, half, jax.ShapeDtypeStruct((NZ, 9 * SLAB, C), BF)],
        in_specs=[SMEM, SMEM] + [VMEM] * 4 + [ANY] * len(pieces),
        out_specs=[VMEM] * 3,
        scratch_shapes=[pltpu.VMEM((960, 3 * C), F32), pltpu.SemaphoreType.DMA((len(pieces),))],
        compiler_params=pltpu.CompilerParams(vmem_limit_bytes=30 * 2**20),
        cost_estimate=cost(960),
        name="conv_first",
    )(tile, where, grown, weight, bias, gain, *pieces)


def slab_rows(weight, tap):
    return weight[:, SLAB * tap : SLAB * (tap + 1)].reshape(3 * C, C)


def finish(lines, start, latent, bias, out, done, sem):
    for i, line in enumerate(lines):
        at = start + 48 * i
        done[48 * i : 48 * i + 48] = (
            line + bias[...] + latent[at : at + 48].astype(F32)
        ).astype(BF)
    copy = pltpu.make_async_copy(done, out.at[pl.ds(start, 288)], sem)
    copy.start()
    copy.wait()


def late_kernel(where, low, high, latent, bias, weight, far, other_far, out, whole, wide, done, sem):
    whole[...] = weight[...]
    for k, src in enumerate((far, other_far)):
        rows = pl.ds(pl.multiple_of(where[3 + 4 * k], BLOCK), BLOCK)
        whole[:, rows] = src[...]
    frames = [part[f] for part in (low, high) for f in range(2)]
    lines = convolve(frames, 3, lambda tap: slab_rows(whole, tap), wide)
    finish(lines, 288, latent, bias, out, done, sem)


def early_kernel(low, high, latent, bias, weight, partial, out, wide, done, sem):
    frames = [part[f] for part in (low, high) for f in range(2)]
    lines = convolve(frames, 3, lambda tap: slab_rows(weight, tap), wide)
    finish(lines, 0, latent, bias, out, done, sem)


SCRATCH = [pltpu.VMEM((288, 3 * C), F32), pltpu.VMEM((288, C), BF)]


def conv_late(where, low, high, latent, bias, weight, far, other_far):
    return pl.pallas_call(
        late_kernel,
        out_shape=[jax.ShapeDtypeStruct((576, C), BF), jax.ShapeDtypeStruct(weight.shape, BF)],
        in_specs=[SMEM] + [VMEM] * 7,
        out_specs=[ANY, VMEM],
        scratch_shapes=[*SCRATCH, pltpu.SemaphoreType.DMA],
        compiler_params=pltpu.CompilerParams(vmem_limit_bytes=20 * 2**20),
        cost_estimate=cost(288),
        name="second_late",
    )(where, low, high, latent, bias, weight, far, other_far)


def conv_early(low, high, latent, bias, weight, partial):
    return pl.pallas_call(
        early_kernel,
        out_shape=jax.ShapeDtypeStruct((576, C), BF),
        in_specs=[VMEM] * 5 + [ANY],
        out_specs=ANY,
        input_output_aliases={5: 0},
        scratch_shapes=[*SCRATCH, pltpu.SemaphoreType.DMA],
        compiler_params=pltpu.CompilerParams(vmem_limit_bytes=12 * 2**20),
        cost_estimate=cost(288),
        name="second_early",
    )(low, high, latent, bias, weight, partial)


def cost(size):
    return pl.CostEstimate(
        flops=2 * size * 27 * C * C, bytes_accessed=27 * C * C * 2, transcendentals=0
    )


def local(latent, gain_first, weight_first, bias_first, gain_second, weight_second, bias_second):
    y, x, z, core = (lax.axis_index(name) for name in AXES)

    def starts(step):
        down, across = lax.rem(y + step + NY, NY), lax.rem(x + step + NX, NX)
        down, across = 2 * BLOCK * down, 2 * BLOCK * across + BLOCK
        return jnp.where(core == 0, down, across), jnp.where(core == 0, across, down)

    mine, other = zip(*(starts(step) for step in (0, -1, 1, 2)))
    where = jnp.stack([*mine, *other]).astype(jnp.int32)
    tile = (y * NX + x).astype(jnp.int32).reshape(1)
    row = lambda v: v.reshape(1, C)

    whole_first = lax.all_gather(weight_first, ("z", "c"), axis=2, tiled=True)
    first = activate(latent, gain_first).astype(BF)
    pieces, far, grown = gather(weight_second.reshape(9, 72, C), y, x, z, core, first)

    second_low, second_high, most = conv_first(
        tile,
        where,
        grown,
        whole_first.reshape(9, 3 * C, C),
        row(bias_first),
        row(gain_second),
        pieces,
    )
    second_earlier = send(second_high, neighbours(0, 1))
    far = after(far, second_high)
    rest = latent.reshape(576, C), row(bias_second)
    partial, whole_second = conv_late(
        where, second_low, second_high, *rest, most, far, send(far, SWAP)
    )
    result = conv_early(second_earlier, second_low, *rest, whole_second, partial)
    return result.reshape(4, 3, 48, C)


def solution(mesh):
    fine = Mesh(mesh.devices.reshape(NY, NX, NZ, 2), AXES)
    frames = P(("z", "c"), ("y", "x"), None, None)
    slices = P(None, None, ("z", "c"), None)
    return jax.shard_map(
        local,
        mesh=fine,
        in_specs=(frames, P(), slices, P(), P(), slices, P()),
        out_specs=frames,
        check_vma=False,
    )
```

```python
import functools

import jax
import jax.numpy as jnp
from jax import lax
from jax.experimental import pallas as pl
from jax.experimental.pallas import tpu as pltpu
from jax.sharding import Mesh
from jax.sharding import PartitionSpec as P

BF = jnp.bfloat16
F32 = jnp.float32
C = 384
NY, NX, NZ = 4, 4, 8
AXES = ("y", "x", "z", "c")
SLAB = 144
PART = 40
BLOCK = 160


def index(y, x, z, c):
    return ((y % NY * NX + x % NX) * NZ + z % NZ) * 2 + c


def perm(to):
    return [
        (index(y, x, z, c), index(*to(y, x, z, c)))
        for y in range(NY)
        for x in range(NX)
        for z in range(NZ)
        for c in range(2)
    ]


def along_z(steps):
    return perm(lambda y, x, z, c: (y, x, z + steps if c == 0 else z - steps, c))


SWAP = perm(lambda y, x, z, c: (y, x, z, 1 - c))
RING_UP = perm(lambda y, x, z, c: (y, x + 1, z, c) if c == 0 else (y + 1, x, z, c))
RING_DOWN = perm(lambda y, x, z, c: (y, x - 1, z, c) if c == 0 else (y - 1, x, z, c))

RING_FAR = perm(lambda y, x, z, c: (y, x + 2, z, c) if c == 0 else (y + 2, x, z, c))
CROSS_UP = perm(lambda y, x, z, c: (y + 1, x, z, c) if c == 0 else (y, x + 1, z, c))
CROSS_FAR = perm(lambda y, x, z, c: (y + 2, x, z, c) if c == 0 else (y, x + 2, z, c))
CROSS_DOWN = perm(lambda y, x, z, c: (y - 1, x, z, c) if c == 0 else (y, x - 1, z, c))


def neighbours(tile_step, group_step):
    tiles, groups = NY * NX, NZ * 2
    return [
        (t * groups + g, (t + tile_step) * groups + g + group_step)
        for t in range(tiles)
        for g in range(groups)
        if 0 <= t + tile_step < tiles and 0 <= g + group_step < groups
    ]


def send(value, pairs):
    return lax.ppermute(value, AXES, pairs)


def activate(values, gain):
    wide = values.astype(F32)
    scaled = wide * lax.rsqrt(jnp.mean(wide * wide, axis=-1, keepdims=True) + 1e-06) * gain
    return jax.nn.silu(scaled)


def after(value, *others):
    return lax.optimization_barrier((value, others))[0]


def grow(own, before):
    own = after(jnp.concatenate([send(own[2:], neighbours(0, 1)), own], axis=0), before)
    above = send(own[:, 1:], neighbours(1, 0))
    below = send(own[:, :2], neighbours(-1, 0))
    return jnp.concatenate([above, own, below], axis=1)


def gather(weight, y, x, z, core, first):
    first_core = core == 0
    other = send(weight, SWAP)
    slab = jnp.concatenate(
        [jnp.where(first_core, weight, other), jnp.where(first_core, other, weight)], axis=1
    ).reshape(9 * SLAB, C)
    starts = BLOCK * 2 * y + PART * x, BLOCK * 2 * x + BLOCK + PART * y
    both = jnp.concatenate(
        [*(lax.dynamic_slice_in_dim(slab, at, PART, axis=0) for at in starts), slab[8 * BLOCK :]],
        axis=0,
    )
    one, two, three, four = (send(both, along_z(steps)) for steps in (1, 2, 3, 4))
    sent = jnp.stack([one, two, three])
    other = send(sent, SWAP)
    plus, minus = jnp.where(first_core, other, sent), jnp.where(first_core, sent, other)
    parts = [both, plus[0], plus[1], plus[2], four, minus[2], minus[1], minus[0]]
    slabs = lax.dynamic_slice_in_dim(jnp.stack(parts + parts), lax.rem(NZ - z, NZ), NZ, axis=0)
    last = slabs[:, 2 * PART :]
    chunk = jnp.where(first_core, slabs[:, :PART], slabs[:, PART : 2 * PART])

    grown = grow(first, both)
    chunk, last = lax.optimization_barrier((chunk, last))
    parts = [chunk, *(send(chunk, pairs) for pairs in (RING_DOWN, RING_FAR, RING_UP))]
    spot = lax.rem(4 - jnp.where(first_core, x, y), 4)
    turned = lax.dynamic_slice_in_dim(jnp.stack(parts + parts), spot, 4, axis=0)
    chunk = turned.transpose(1, 0, 2, 3).reshape(NZ, BLOCK, C)
    chunk = after(chunk, grown)
    up, down = send(chunk, CROSS_UP), send(chunk, CROSS_DOWN)
    far = send(after(chunk, up, down), CROSS_FAR)
    others = [send(v, SWAP) for v in (chunk, up, down)]
    return [chunk, up, down, *others, last], far, grown


ANY = pl.BlockSpec(memory_space=pl.ANY)
VMEM = pl.BlockSpec(memory_space=pltpu.VMEM)
SMEM = pl.BlockSpec(memory_space=pltpu.SMEM)


def convolve(frames, rows, whole, wide):
    count = len(frames) - 2

    def left(t, k):
        shown = [frames[t + f][k : k + rows].reshape(rows * 48, C) for f in range(count)]
        return jnp.concatenate(shown, axis=0)

    def right(t, k):
        tap = whole(3 * t + k)
        return jnp.concatenate([tap[d * C : (d + 1) * C] for d in range(3)], axis=1)

    taps = [(t, k) for t in range(3) for k in range(3)]
    wide[...] = jnp.dot(
        jnp.concatenate([left(t, k) for t, k in taps], axis=1),
        jnp.concatenate([right(t, k) for t, k in taps], axis=0),
        preferred_element_type=F32,
    )
    column = lax.broadcasted_iota(jnp.int32, (48, C), 0)
    lines = []
    for i in range(count * rows):
        line = wide[48 * i : 48 * i + 48]
        before = jnp.where(column == 0, 0.0, pltpu.roll(line[:, :C], 1, 0))
        behind = jnp.where(column == 47, 0.0, pltpu.roll(line[:, 2 * C :], 47, 0))
        lines.append(before + line[:, C : 2 * C] + behind)
    return lines


def first_kernel(tile, where, grown, weight, bias, gain, *refs):
    *arrays, last, out_low, out_high, next_weight, wide, sems = refs
    copies = []
    for k, src in enumerate([*arrays, last]):
        if src is last:
            rows = pl.ds(8 * BLOCK, 9 * SLAB - 8 * BLOCK)
        else:
            rows = pl.ds(pl.multiple_of(where[k + k // 3], BLOCK), BLOCK)
        copies.append(pltpu.make_async_copy(src, next_weight.at[:, rows], sems.at[k]))
        copies[k].start()
    lines = convolve([grown[f] for f in range(6)], 5, lambda tap: weight[tap], wide)
    for i, line in enumerate(lines):
        result = activate(line + bias[...], gain[...])
        if i % 5 == 0:
            result = jnp.where(tile[0] == 0, 0.0, result)
        if i % 5 == 4:
            result = jnp.where(tile[0] == NY * NX - 1, 0.0, result)
        out = out_low if i < 10 else out_high
        out[i // 5 % 2, i % 5] = result.astype(BF)
    for copy in copies:
        copy.wait()


def conv_first(tile, where, grown, weight, bias, gain, pieces):
    half = jax.ShapeDtypeStruct((2, 5, 48, C), BF)
    return pl.pallas_call(
        first_kernel,
        out_shape=[half, half, jax.ShapeDtypeStruct((NZ, 9 * SLAB, C), BF)],
        in_specs=[SMEM, SMEM] + [VMEM] * 4 + [ANY] * len(pieces),
        out_specs=[VMEM] * 3,
        scratch_shapes=[pltpu.VMEM((960, 3 * C), F32), pltpu.SemaphoreType.DMA((len(pieces),))],
        compiler_params=pltpu.CompilerParams(vmem_limit_bytes=38 * 2**20),
        cost_estimate=cost(960),
        name="conv_first",
    )(tile, where, grown, weight, bias, gain, *pieces)


def slab_rows(weight, tap):
    return weight[:, SLAB * tap : SLAB * (tap + 1)].reshape(3 * C, C)


def finish(lines, start, latent, bias, out, done, sem):
    for i, line in enumerate(lines):
        at = start + 48 * i
        done[48 * i : 48 * i + 48] = (
            line + bias[...] + latent[at : at + 48].astype(F32)
        ).astype(BF)
    copy = pltpu.make_async_copy(done, out.at[pl.ds(start, 288)], sem)
    copy.start()
    copy.wait()


def late_kernel(where, low, high, latent, bias, weight, far, other_far, out, whole, wide, done, sem):
    whole[...] = weight[...]
    for k, src in enumerate((far, other_far)):
        rows = pl.ds(pl.multiple_of(where[3 + 4 * k], BLOCK), BLOCK)
        whole[:, rows] = src[...]
    frames = [part[f] for part in (low, high) for f in range(2)]
    lines = convolve(frames, 3, lambda tap: slab_rows(whole, tap), wide)
    finish(lines, 288, latent, bias, out, done, sem)


def early_kernel(low, high, latent, bias, weight, partial, out, wide, done, sem):
    frames = [part[f] for part in (low, high) for f in range(2)]
    lines = convolve(frames, 3, lambda tap: slab_rows(weight, tap), wide)
    finish(lines, 0, latent, bias, out, done, sem)


SCRATCH = [pltpu.VMEM((288, 3 * C), F32), pltpu.VMEM((288, C), BF)]


def conv_late(where, low, high, latent, bias, weight, far, other_far):
    return pl.pallas_call(
        late_kernel,
        out_shape=[jax.ShapeDtypeStruct((576, C), BF), jax.ShapeDtypeStruct(weight.shape, BF)],
        in_specs=[SMEM] + [VMEM] * 7,
        out_specs=[ANY, VMEM],
        scratch_shapes=[*SCRATCH, pltpu.SemaphoreType.DMA],
        compiler_params=pltpu.CompilerParams(vmem_limit_bytes=20 * 2**20),
        cost_estimate=cost(288),
        name="second_late",
    )(where, low, high, latent, bias, weight, far, other_far)


def conv_early(low, high, latent, bias, weight, partial):
    return pl.pallas_call(
        early_kernel,
        out_shape=jax.ShapeDtypeStruct((576, C), BF),
        in_specs=[VMEM] * 5 + [ANY],
        out_specs=ANY,
        input_output_aliases={5: 0},
        scratch_shapes=[*SCRATCH, pltpu.SemaphoreType.DMA],
        compiler_params=pltpu.CompilerParams(vmem_limit_bytes=12 * 2**20),
        cost_estimate=cost(288),
        name="second_early",
    )(low, high, latent, bias, weight, partial)


def cost(size):
    return pl.CostEstimate(
        flops=2 * size * 27 * C * C, bytes_accessed=27 * C * C * 2, transcendentals=0
    )


def local(latent, gain_first, weight_first, bias_first, gain_second, weight_second, bias_second):
    y, x, z, core = (lax.axis_index(name) for name in AXES)

    def starts(step):
        down, across = lax.rem(y + step + NY, NY), lax.rem(x + step + NX, NX)
        down, across = 2 * BLOCK * down, 2 * BLOCK * across + BLOCK
        return jnp.where(core == 0, down, across), jnp.where(core == 0, across, down)

    mine, other = zip(*(starts(step) for step in (0, -1, 1, 2)))
    where = jnp.stack([*mine, *other]).astype(jnp.int32)
    tile = (y * NX + x).astype(jnp.int32).reshape(1)
    row = lambda v: v.reshape(1, C)

    whole_first = lax.all_gather(weight_first, ("z", "c"), axis=2, tiled=True)
    first = activate(latent, gain_first).astype(BF)
    pieces, far, grown = gather(weight_second.reshape(9, 72, C), y, x, z, core, first)

    second_low, second_high, most = conv_first(
        tile,
        where,
        grown,
        whole_first.reshape(9, 3 * C, C),
        row(bias_first),
        row(gain_second),
        pieces,
    )
    second_earlier = send(second_high, neighbours(0, 1))
    far = after(far, second_high)
    rest = latent.reshape(576, C), row(bias_second)
    partial, whole_second = conv_late(
        where, second_low, second_high, *rest, most, far, send(far, SWAP)
    )
    result = conv_early(second_earlier, second_low, *rest, whole_second, partial)
    return result.reshape(4, 3, 48, C)


def solution(mesh):
    fine = Mesh(mesh.devices.reshape(NY, NX, NZ, 2), AXES)
    frames = P(("z", "c"), ("y", "x"), None, None)
    slices = P(None, None, ("z", "c"), None)
    return jax.shard_map(
        local,
        mesh=fine,
        in_specs=(frames, P(), slices, P(), P(), slices, P()),
        out_specs=frames,
        check_vma=False,
    )
```
